32 devices in a mesh: dp: 8 (over z, x), heads: 4 (over y, core).
Axes of the slice: x: 2, y: 2, z: 4, core: 2. Of those that a mesh axis runs over, the one named last changes fastest.
Arguments:
- small_tokens: bfloat16 [128, 196, 192], P('dp'), may hold values from -6 to 6
- large_tokens: bfloat16 [128, 145, 384], P('dp'), may hold values from -6 to 6
- small_cotangent: bfloat16 [128, 196, 192], P('dp'), may hold values from -6 to 6
- large_cotangent: bfloat16 [128, 145, 384], P('dp'), may hold values from -6 to 6
- small_gain_attn: float32 [192], replicated, may hold values from 0.1 to 1.9
- small_qkv: bfloat16 [192, 576], replicated, may hold values from -0.4375 to 0.4375
- small_out: bfloat16 [192, 192], replicated, may hold values from -1.25 to 1.25
- small_gain_mlp: float32 [192], replicated, may hold values from 0.1 to 1.9
- small_up: bfloat16 [192, 768], P(None, 'heads'), may hold values from -0.4375 to 0.4375
- small_down: bfloat16 [768, 192], P('heads'), may hold values from -0.21875 to 0.21875
- large_gain_attn: float32 [4, 384], replicated, may hold values from 0.1 to 1.9
- large_qkv: bfloat16 [4, 384, 1152], replicated, may hold values from -0.3125 to 0.3125
- large_out: bfloat16 [4, 384, 384], replicated, may hold values from -0.875 to 0.875
- large_gain_mlp: float32 [4, 384], replicated, may hold values from 0.1 to 1.9
- large_up: bfloat16 [4, 384, 1536], P(None, None, 'heads'), may hold values from -0.3125 to 0.3125
- large_down: bfloat16 [4, 1536, 384], P(None, 'heads'), may hold values from -0.15625 to 0.15625
- unite_small_gain_in: float32 [192], replicated, may hold values from 0.1 to 1.9
- unite_small_lift: bfloat16 [192, 384], replicated, may hold values from -0.4375 to 0.4375
- unite_small_gain_attn: float32 [384], replicated, may hold values from 0.1 to 1.9
- unite_small_qkv: bfloat16 [384, 1152], replicated, may hold values from -0.3125 to 0.3125
- unite_small_out: bfloat16 [384, 384], replicated, may hold values from -0.875 to 0.875
- unite_small_gain_back: float32 [384], replicated, may hold values from 0.1 to 1.9
- unite_small_revert: bfloat16 [384, 192], replicated, may hold values from -0.3125 to 0.3125
- unite_large_gain_in: float32 [384], replicated, may hold values from 0.1 to 1.9
- unite_large_lift: bfloat16 [384, 192], replicated, may hold values from -0.3125 to 0.3125
- unite_large_gain_attn: float32 [192], replicated, may hold values from 0.1 to 1.9
- unite_large_qkv: bfloat16 [192, 576], replicated, may hold values from -0.4375 to 0.4375
- unite_large_out: bfloat16 [192, 192], replicated, may hold values from -1.25 to 1.25
- unite_large_gain_back: float32 [192], replicated, may hold values from 0.1 to 1.9
- unite_large_revert: bfloat16 [192, 384], replicated, may hold values from -0.4375 to 0.4375
Outputs:
- small_result: bfloat16 [128, 196, 192], P('dp')
- large_result: bfloat16 [128, 145, 384], P('dp')
- small_grad: float32 [128, 196, 192], P('dp')
- large_grad: float32 [128, 145, 384], P('dp')
- grad_small_gain_attn: float32 [192], replicated
- grad_small_qkv: float32 [192, 576], replicated
- grad_small_out: float32 [192, 192], replicated
- grad_small_gain_mlp: float32 [192], replicated
- grad_small_up: float32 [192, 768], P(None, 'heads')
- grad_small_down: float32 [768, 192], P('heads')
- grad_large_gain_attn: float32 [4, 384], replicated
- grad_large_qkv: float32 [4, 384, 1152], replicated
- grad_large_out: float32 [4, 384, 384], replicated
- grad_large_gain_mlp: float32 [4, 384], replicated
- grad_large_up: float32 [4, 384, 1536], P(None, None, 'heads')
- grad_large_down: float32 [4, 1536, 384], P(None, 'heads')
- grad_unite_small_gain_in: float32 [192], replicated
- grad_unite_small_lift: float32 [192, 384], replicated
- grad_unite_small_gain_attn: float32 [384], replicated
- grad_unite_small_qkv: float32 [384, 1152], replicated
- grad_unite_small_out: float32 [384, 384], replicated
- grad_unite_small_gain_back: float32 [384], replicated
- grad_unite_small_revert: float32 [384, 192], replicated
- grad_unite_large_gain_in: float32 [384], replicated
- grad_unite_large_lift: float32 [384, 192], replicated
- grad_unite_large_gain_attn: float32 [192], replicated
- grad_unite_large_qkv: float32 [192, 576], replicated
- grad_unite_large_out: float32 [192, 192], replicated
- grad_unite_large_gain_back: float32 [192], replicated
- grad_unite_large_revert: float32 [192, 384], replicated
The draws below stay inside these ranges and needn't reach their ends.
All inputs are finite; a program needn't handle non-finite values.
Results may differ from the reference program's by a relative error of at most 0.025.
Values may be sent and summed in bfloat16 or wider, within the bound.
No kernel may reach another device: no remote copies, remote signals or barrier semaphores. Data moves between devices by JAX's collectives and lax.ppermute only.
A program may use at most 384 MiB of HBM per device.

```python
import jax
import jax.numpy as jnp
from jax import lax

DS = 192
DL = 384
MS = 768
ML = 1536
HEADS = 6
LDEPTH = 4
NS = 196
NL = 145
IMG_DEV = 16
IMAGES = 128


def block_scale(rng, extent, cuts, low, largest):
    loudness = 1.0
    for position, shards_of in cuts:
        heights = jax.random.uniform(jax.random.fold_in(jax.random.fold_in(rng, 6), position), (shards_of,), jnp.float32, low / len(cuts), largest / len(cuts))
        loudness = loudness * jnp.repeat(jnp.exp(heights), extent[position] // shards_of).reshape((-1,) + (1,) * (len(extent) - 1 - position))
    return loudness


def centred(stream_key, dims, scale, most, shards=(), dtype=jnp.bfloat16):
    level = block_scale(stream_key, dims, shards, -0.22, 0.18) if shards else 1.0
    values = jax.random.normal(stream_key, dims, jnp.float32) * scale * level
    return jnp.minimum(jnp.maximum(values, -most), most).astype(dtype)


def setup_inputs(seed: int = 0) -> dict:
    arg_keys = jax.random.split(jax.random.key(seed), 31)
    small_tokens = centred(arg_keys[0], (IMAGES, NS, DS), 1.0, 6.0, ((0, 8),))
    large_tokens = centred(arg_keys[1], (IMAGES, NL, DL), 1.0, 6.0, ((0, 8),))
    small_cotangent = centred(arg_keys[2], (IMAGES, NS, DS), 1.0, 6.0, ((0, 8),))
    large_cotangent = centred(arg_keys[3], (IMAGES, NL, DL), 1.0, 6.0, ((0, 8),))
    small_gain_attn = jnp.clip(1.0 + 0.18 * jax.random.normal(arg_keys[4], (DS,), jnp.float32), 0.1, 1.9)
    small_qkv = centred(arg_keys[5], (DS, 3 * DS), DS ** -0.5, 0.4375)
    small_out = centred(arg_keys[6], (DS, DS), (DS // 8) ** -0.5, 1.25)
    small_gain_mlp = jnp.clip(1.0 + 0.18 * jax.random.normal(arg_keys[7], (DS,), jnp.float32), 0.1, 1.9)
    small_up = centred(arg_keys[8], (DS, MS), DS ** -0.5, 0.4375, ((1, 4),))
    small_down = centred(arg_keys[9], (MS, DS), MS ** -0.5, 0.21875, ((0, 4),))
    large_gain_attn = jnp.clip(1.0 + 0.18 * jax.random.normal(arg_keys[10], (LDEPTH, DL), jnp.float32), 0.1, 1.9)
    large_qkv = centred(arg_keys[11], (LDEPTH, DL, 3 * DL), DL ** -0.5, 0.3125)
    large_out = centred(arg_keys[12], (LDEPTH, DL, DL), (DL // 8) ** -0.5, 0.875)
    large_gain_mlp = jnp.clip(1.0 + 0.18 * jax.random.normal(arg_keys[13], (LDEPTH, DL), jnp.float32), 0.1, 1.9)
    large_up = centred(arg_keys[14], (LDEPTH, DL, ML), DL ** -0.5, 0.3125, ((2, 4),))
    large_down = centred(arg_keys[15], (LDEPTH, ML, DL), ML ** -0.5, 0.15625, ((1, 4),))
    unite_small_gain_in = jnp.clip(1.0 + 0.18 * jax.random.normal(arg_keys[16], (DS,), jnp.float32), 0.1, 1.9)
    unite_small_lift = centred(arg_keys[17], (DS, DL), DS ** -0.5, 0.4375)
    unite_small_gain_attn = jnp.clip(1.0 + 0.18 * jax.random.normal(arg_keys[18], (DL,), jnp.float32), 0.1, 1.9)
    unite_small_qkv = centred(arg_keys[19], (DL, 3 * DL), DL ** -0.5, 0.3125)
    unite_small_out = centred(arg_keys[20], (DL, DL), (DL // 8) ** -0.5, 0.875)
    unite_small_gain_back = jnp.clip(1.0 + 0.18 * jax.random.normal(arg_keys[21], (DL,), jnp.float32), 0.1, 1.9)
    unite_small_revert = centred(arg_keys[22], (DL, DS), DL ** -0.5, 0.3125)
    unite_large_gain_in = jnp.clip(1.0 + 0.18 * jax.random.normal(arg_keys[23], (DL,), jnp.float32), 0.1, 1.9)
    unite_large_lift = centred(arg_keys[24], (DL, DS), DL ** -0.5, 0.3125)
    unite_large_gain_attn = jnp.clip(1.0 + 0.18 * jax.random.normal(arg_keys[25], (DS,), jnp.float32), 0.1, 1.9)
    unite_large_qkv = centred(arg_keys[26], (DS, 3 * DS), DS ** -0.5, 0.4375)
    unite_large_out = centred(arg_keys[27], (DS, DS), (DS // 8) ** -0.5, 1.25)
    unite_large_gain_back = jnp.clip(1.0 + 0.18 * jax.random.normal(arg_keys[28], (DS,), jnp.float32), 0.1, 1.9)
    unite_large_revert = centred(arg_keys[29], (DS, DL), DS ** -0.5, 0.4375)
    return {"small_tokens": small_tokens, "large_tokens": large_tokens, "small_cotangent": small_cotangent, "large_cotangent": large_cotangent, "small_gain_attn": small_gain_attn, "small_qkv": small_qkv, "small_out": small_out, "small_gain_mlp": small_gain_mlp, "small_up": small_up, "small_down": small_down, "large_gain_attn": large_gain_attn, "large_qkv": large_qkv, "large_out": large_out, "large_gain_mlp": large_gain_mlp, "large_up": large_up, "large_down": large_down, "unite_small_gain_in": unite_small_gain_in, "unite_small_lift": unite_small_lift, "unite_small_gain_attn": unite_small_gain_attn, "unite_small_qkv": unite_small_qkv, "unite_small_out": unite_small_out, "unite_small_gain_back": unite_small_gain_back, "unite_small_revert": unite_small_revert, "unite_large_gain_in": unite_large_gain_in, "unite_large_lift": unite_large_lift, "unite_large_gain_attn": unite_large_gain_attn, "unite_large_qkv": unite_large_qkv, "unite_large_out": unite_large_out, "unite_large_gain_back": unite_large_gain_back, "unite_large_revert": unite_large_revert}


EPS = 1e-06
HIGH = lax.Precision.HIGHEST

@jax.custom_vjp
def low(v):
    return lax.optimization_barrier(v.astype(jnp.bfloat16)).astype(jnp.float32)

@jax.custom_vjp
def low_back(v):
    return v

def low_keep(v):
    return (low(v), None)

def low_pass(kept, grad):
    return (grad,)

def back_keep(v):
    return (v, None)

def back_low(kept, grad):
    return (low(grad),)
low.defvjp(low_keep, low_pass)
low_back.defvjp(back_keep, back_low)

def product(form, left, right):
    return jnp.einsum(form, left, right, precision=HIGH)

def layer_norm(values, gain):
    center = values - lax.optimization_barrier(jnp.mean(values, axis=-1, keepdims=True))
    spread = lax.optimization_barrier(jnp.mean(center * center, axis=-1, keepdims=True))
    return center * lax.rsqrt(spread + EPS) * gain

def exact_gelu(values):
    return jax.nn.gelu(values, approximate=False)

def block(tokens, weights):
    gain_attn, qkv, out, gain_mlp, up, down = weights
    images, length, width = tokens.shape
    head_size = width // HEADS
    normed = low(layer_norm(tokens, gain_attn))
    mixed = low(low_back(product('gnd,de->gne', normed, qkv))).reshape(images, length, 3, HEADS, head_size)
    scores = low_back(product('gqhe,gkhe->ghqk', mixed[:, :, 0], mixed[:, :, 1]) * head_size ** (-0.5))
    probs = low(jax.nn.softmax(scores, axis=-1))
    heads = low(low_back(product('ghqk,gkhe->gqhe', probs, mixed[:, :, 2]).reshape(images, length, width)))
    middle = tokens + low_back(product('gnd,de->gne', heads, out))
    normed_mlp = low(layer_norm(middle, gain_mlp))
    inner = low_back(product('gnd,de->gne', normed_mlp, up))
    active = low(exact_gelu(inner))
    return middle + low_back(product('gnd,de->gne', active, down))

def unite(cls_rows, patches, weights):
    gain_in, lift, gain_attn, qkv, out, gain_back, revert = weights
    images, count, width = patches.shape
    head_size = width // HEADS
    lifted_in = low(exact_gelu(layer_norm(cls_rows, gain_in)))
    lifted = low_back(product('gd,de->ge', lifted_in, lift))
    joined = jnp.concatenate([lifted[:, None], patches], axis=1)
    normed = low(layer_norm(joined, gain_attn))
    query = low(low_back(product('gd,de->ge', normed[:, 0], qkv[:, :width]))).reshape(images, HEADS, head_size)
    keyval = low(low_back(product('gnd,de->gne', normed, qkv[:, width:]))).reshape(images, count + 1, 2, HEADS, head_size)
    scores = low_back(product('ghe,gkhe->ghk', query, keyval[:, :, 0]) * head_size ** (-0.5))
    probs = low(jax.nn.softmax(scores, axis=-1))
    heads = low(low_back(product('ghk,gkhe->ghe', probs, keyval[:, :, 1]).reshape(images, width)))
    calibrated = lifted + low_back(product('gd,de->ge', heads, out))
    back_in = low(exact_gelu(layer_norm(calibrated, gain_back)))
    return low_back(product('gd,de->ge', back_in, revert))

def group_forward(weights, small_in, large_in):
    small_mid = block(small_in, weights[0:6])
    large_mid = large_in
    for layer in range(LDEPTH):
        large_mid = block(large_mid, tuple((weight[layer] for weight in weights[6:12])))
    small_head = unite(small_mid[:, 0], large_mid[:, 1:], weights[12:19])
    large_head = unite(large_mid[:, 0], small_mid[:, 1:], weights[19:26])
    small_out = jnp.concatenate([small_head[:, None], small_mid[:, 1:]], axis=1)
    large_out = jnp.concatenate([large_head[:, None], large_mid[:, 1:]], axis=1)
    return (small_out, large_out)

def reference(small_tokens, large_tokens, small_cotangent, large_cotangent, small_gain_attn, small_qkv, small_out, small_gain_mlp, small_up, small_down, large_gain_attn, large_qkv, large_out, large_gain_mlp, large_up, large_down, unite_small_gain_in, unite_small_lift, unite_small_gain_attn, unite_small_qkv, unite_small_out, unite_small_gain_back, unite_small_revert, unite_large_gain_in, unite_large_lift, unite_large_gain_attn, unite_large_qkv, unite_large_out, unite_large_gain_back, unite_large_revert):
    listed = (small_gain_attn, small_qkv, small_out, small_gain_mlp, small_up, small_down, large_gain_attn, large_qkv, large_out, large_gain_mlp, large_up, large_down, unite_small_gain_in, unite_small_lift, unite_small_gain_attn, unite_small_qkv, unite_small_out, unite_small_gain_back, unite_small_revert, unite_large_gain_in, unite_large_lift, unite_large_gain_attn, unite_large_qkv, unite_large_out, unite_large_gain_back, unite_large_revert)
    weights = tuple((array.astype(jnp.float32) for array in listed))
    groups = small_tokens.shape[0] // IMG_DEV

    def forward(params, small_all, large_all):
        small_split = small_all.reshape(groups, IMG_DEV, NS, DS)
        large_split = large_all.reshape(groups, IMG_DEV, NL, DL)

        def one_group(pair):
            return group_forward(params, pair[0], pair[1])
        small_res, large_res = lax.map(jax.checkpoint(one_group), (small_split, large_split))
        return (small_res.reshape(-1, NS, DS), large_res.reshape(-1, NL, DL))
    outputs, pull = jax.vjp(forward, weights, small_tokens.astype(jnp.float32), large_tokens.astype(jnp.float32))
    grads, small_grad, large_grad = pull((small_cotangent.astype(jnp.float32), large_cotangent.astype(jnp.float32)))
    return (outputs[0].astype(jnp.bfloat16), outputs[1].astype(jnp.bfloat16), small_grad, large_grad, grads[0], grads[1], grads[2], grads[3], grads[4], grads[5], grads[6], grads[7], grads[8], grads[9], grads[10], grads[11], grads[12], grads[13], grads[14], grads[15], grads[16], grads[17], grads[18], grads[19], grads[20], grads[21], grads[22], grads[23], grads[24], grads[25])
```

```python
import collections
import functools
import types

import jax
import jax.numpy as jnp
from jax import lax
from jax.experimental import pallas as pl
from jax.experimental.pallas import tpu as pltpu
from jax.sharding import PartitionSpec as P

HEADS_AXIS, ROW_AXIS = "heads", "dp"
MIDDLE, RESULT, Y_OUT, GRAD_X = "middle_out", "result_out", "y_out", "grad_x_out"
KEEP, SEND, GAIN_ATTN, GAIN_MLP = "keep_out", "send_out", "gain_attn_out", "gain_mlp_out"
EPS = 1e-06
SINGLE = jnp.float32
HALF = jnp.bfloat16
HEADS = 6
LANES = 128
WINDOW = 256
CLS_ROWS = 16
NEG = -1e30
ROOT_HALF = 0.7071067811865476
INV_ROOT_2PI = 0.3989422804014327
VMEM_BYTES = 60 * 1024 * 1024
FORWARD_UNROLL = 4
LINE_ROWS = 16
BACKWARD_UNROLL = 4

Branch = collections.namedtuple("Branch", ("images", "rows", "length", "width", "true", "hidden"))


def round_up(value, step):
    return -(-value // step) * step


def dot(left, right):
    return jnp.dot(left, right, preferred_element_type=SINGLE)


def dot_nt(left, right):
    return lax.dot_general(left, right, (((1,), (1,)), ((), ())), preferred_element_type=SINGLE)


def dot_tn(left, right):
    return lax.dot_general(left, right, (((0,), (0,)), ((), ())), preferred_element_type=SINGLE)


def iota(shape, dim):
    return lax.broadcasted_iota(jnp.int32, shape, dim)


def norm(values, true):
    width = values.shape[-1]
    mean = jnp.sum(values, axis=-1, keepdims=True) * (1.0 / true)
    center = values - mean
    if true != width:
        center = jnp.where(iota((1, width), 1) < true, center, 0.0)
    spread = jnp.sum(center * center, axis=-1, keepdims=True) * (1.0 / true)
    scale = lax.rsqrt(spread + EPS)
    return center * scale, scale


def norm_back(grad, unit, scale, true):
    mean = jnp.sum(grad, axis=-1, keepdims=True) * (1.0 / true)
    along = jnp.sum(grad * unit, axis=-1, keepdims=True) * (1.0 / true)
    return scale * (grad - mean - unit * along)


def gelu_both(values):
    phi = 0.5 + 0.5 * lax.erf(values * ROOT_HALF)
    density = jnp.exp(values * values * -0.5) * INV_ROOT_2PI
    return values * phi, phi + values * density


def heads_of(cfg, block):
    size = cfg.true // HEADS
    per = LANES // size
    first = block * per
    return size, [head for head in range(first, min(first + per, HEADS))]


def lane_mask(head, size):
    low = head * size % LANES
    lane = iota((1, LANES), 1)
    return (lane >= low) & (lane < low + size)


class Copies:
    def __init__(self, semaphores):
        self.semaphores, self.used, self.puts = semaphores, 0, []

    def begin(self, source, target):
        copy = pltpu.make_async_copy(source, target, self.semaphores.at[self.used])
        self.used += 1
        copy.start()
        return copy

    def put(self, source, target):
        self.puts.append(self.begin(source, target))

    def block(self, count):
        self.used += count
        return self.used - count

    def finish(self):
        for copy in self.puts:
            copy.wait()


def wait(copies):
    for copy in copies:
        copy.wait()


def flipped(cfg):
    return cfg.true != cfg.width


def tokens_shape(cfg):
    return (cfg.images, cfg.true, cfg.length) if flipped(cfg) else (cfg.images, cfg.length, cfg.true)


def put_tokens(cfg, target, image, rows):
    rows = rows.T if flipped(cfg) else rows
    target[image] = rows[0 : target.shape[1], 0 : target.shape[2]].astype(HALF)


def load_tokens(cfg, place, tokens, landing, target, copies):
    copy = copies.begin(tokens.at[pl.ds(place[0] * cfg.images, cfg.images)], landing)
    target[...] = jnp.zeros(target.shape, target.dtype)
    copy.wait()
    for image in range(cfg.images):
        first = image * cfg.rows
        rows = landing[image].astype(target.dtype)
        target[first : first + cfg.length, 0 : cfg.true] = rows.T if flipped(cfg) else rows


def shard_copies(cfg, copies, shards, target, index):
    size = cfg.hidden // 4
    gets = []
    for number, shard in enumerate(shards):
        part = slice(number * size, (number + 1) * size)
        gets.append(copies.begin(shard.at[index], target.at[:, part] if index == 0 else target.at[part, :]))
    return gets


def rows_of(cfg, image):
    return pl.ds(pl.multiple_of(image * cfg.rows, 16), cfg.rows)


def attention(cfg, mixed, heads, probs, image, key_ok, query_ok):
    rows, width = cfg.rows, cfg.width
    work = []
    for block in range(width // LANES):
        low = block * LANES
        base = pl.multiple_of(image * rows, 16)
        query = mixed[pl.ds(base, WINDOW), low : low + LANES]
        key = mixed[pl.ds(base, rows), width + low : width + low + LANES]
        size, here = heads_of(cfg, block)
        for head in here:
            masked = jnp.where(lane_mask(head, size), key, jnp.zeros_like(key))
            work.append(dot_nt(masked, query))
    order = 0
    for block in range(width // LANES):
        low = block * LANES
        base = pl.multiple_of(image * rows, 16)
        value_t = mixed[pl.ds(base, rows), 2 * width + low : 2 * width + low + LANES].T
        size, here = heads_of(cfg, block)
        pieces = []
        for head in here:
            scores = jnp.where(key_ok, work[order] * size ** (-0.5), NEG)
            order += 1
            top = jnp.max(scores, axis=0, keepdims=True)
            raised = jnp.exp(scores - top)
            total_row = jnp.sum(raised, axis=0, keepdims=True)
            prob = (raised * (query_ok / total_row)).astype(HALF)
            probs[image * HEADS + head] = prob
            first = head * size % LANES
            pieces.append(dot(value_t[first : first + size], prob))
        if len(here) * size < LANES:
            pieces.append(jnp.zeros((LANES - len(here) * size, WINDOW), SINGLE))
        heads[pl.ds(base, rows), low : low + LANES] = jnp.concatenate(pieces, axis=0).T[:rows].astype(HALF)


def forward_attn(cfg, r, copies, get_x, get_qkv, get_out):
    rows, width = cfg.rows, cfg.width
    total = cfg.images * rows
    wait(get_x)

    @pl.loop(0, cfg.images)
    def _(image):
        at = rows_of(cfg, image)
        unit, _ = norm(r.x[at, :], cfg.true)
        r.normed[at, :] = (unit * r.gain_attn[...]).astype(HALF)

    wait(get_qkv)
    for part in range(3):
        cols = slice(part * width, (part + 1) * width)
        r.mixed[0:total, cols] = dot(r.normed[...], r.qkv[:, cols]).astype(HALF)
    r.mixed[total:, :] = jnp.zeros((r.mixed.shape[0] - total, 3 * width), HALF)
    copies.put(r.mixed, r.mixed_out)

    key_ok = iota((rows, WINDOW), 0) < cfg.length
    query_ok = (iota((1, WINDOW), 1) < cfg.length).astype(SINGLE)

    @pl.loop(0, cfg.images // FORWARD_UNROLL)
    def _(step):
        for part in range(FORWARD_UNROLL):
            attention(cfg, r.mixed, r.heads, r.probs, step * FORWARD_UNROLL + part, key_ok, query_ok)

    copies.put(r.probs, r.probs_out)
    copies.put(r.heads, r.heads_out)
    wait(get_out)
    r.middle[...] = r.x[...] + dot(r.heads[...], r.out[...])
    copies.put(r.middle, r.middle_out)


def forward_mlp(cfg, r, copies, get_middle, get_up, get_down):
    first = copies.block(2 * cfg.images)
    wait(get_middle + get_up)

    def puts(image):
        at = rows_of(cfg, image)
        return [
            pltpu.make_async_copy(r.active.at[at], r.active_out.at[at], copies.semaphores.at[first + 2 * image]),
            pltpu.make_async_copy(r.slope.at[at], r.slope_out.at[at], copies.semaphores.at[first + 2 * image + 1]),
        ]

    @pl.loop(0, cfg.images)
    def _(image):
        at = rows_of(cfg, image)
        unit, _ = norm(r.middle[at, :], cfg.true)
        normed = (unit * r.gain_mlp[...]).astype(HALF)
        for low in range(0, cfg.hidden, WINDOW):
            cols = slice(low, low + WINDOW)
            act, grad = gelu_both(dot(normed, r.up[:, cols]))
            r.active[at, cols] = act.astype(HALF)
            r.slope[at, cols] = grad.astype(HALF)
        for copy in puts(image):
            copy.start()

    wait(get_down)
    half = cfg.images * cfg.rows // 2
    for part in range(2):
        at = slice(part * half, (part + 1) * half)
        r.y[at, :] = r.middle[at, :] + dot(r.active[at, :], r.down[...])
        copies.put(r.y.at[at], r.y_out.at[at])
    for image in range(cfg.images):
        wait(puts(image))


def pick_layer(layer, r):
    if layer is not None and hasattr(r, "qkv_in"):
        r.qkv_in, r.out_in = r.qkv_in.at[layer], r.out_in.at[layer]


def forward_body(cfg, layer, attn, mlp, r):
    pick_layer(layer, r)
    copies = Copies(r.semaphores)
    get_x = get_middle = get_up = get_down = []
    if attn:
        if hasattr(r, "tokens"):
            load_tokens(cfg, r.place, r.tokens, r.landing, r.x, copies)
            copies.put(r.x, r.x_out)
        else:
            get_x = [copies.begin(r.x_in, r.x)]
        get_qkv = [copies.begin(r.qkv_in, r.qkv)]
        get_out = [copies.begin(r.out_in, r.out)]
    else:
        get_middle = [copies.begin(r.middle_in, r.middle)]
    if mlp:
        shards = (r.own, r.core, r.far, r.both)
        get_up = shard_copies(cfg, copies, shards, r.up, 0)
        get_down = shard_copies(cfg, copies, shards, r.down, 1)
    if attn:
        forward_attn(cfg, r, copies, get_x, get_qkv, get_out)
    if mlp:
        forward_mlp(cfg, r, copies, get_middle, get_up, get_down)
    copies.finish()


def backward_mlp(cfg, r, copies, get):
    rows, width = cfg.rows, cfg.width
    size = cfg.hidden // 4
    wait(get["grad"])
    r.branch[...] = r.grad[...].astype(HALF)
    wait(get["down"] + get["slope"])

    @pl.loop(0, cfg.images)
    def _(image):
        at = rows_of(cfg, image)
        for low in range(0, cfg.hidden, WINDOW):
            cols = slice(low, low + WINDOW)
            grad_active = dot_nt(r.branch[at, :], r.down[cols, :])
            r.inner[at, cols] = (grad_active * r.slope[at, cols].astype(SINGLE)).astype(HALF)

    def put(index):
        for shard in range(4):
            target = (r.keep_out, r.send_out)[shard % 2]
            cols = slice(shard * size, (shard + 1) * size)
            if cfg.true == width:
                chunk = target.at[shard // 2 * 2 + lax.rem(r.place[1] + index, 2), 0:width]
                copies.put(r.pieces_mlp.at[index, :, cols], chunk)
            else:
                at = slice(index * cfg.true, (index + 1) * cfg.true)
                r.packed[shard, :, at] = r.pieces_mlp[index, 0 : cfg.true, cols][:, 0 : cfg.true]
                if index == 0:
                    half = cfg.true // 2
                    for side in range(2):
                        chunk = shard // 2 * 2 + lax.rem(r.place[1] + side, 2)
                        rows_here = slice(side * half, (side + 1) * half)
                        copies.put(r.packed.at[shard, rows_here], target.at[chunk, 0:half])

    wait(get["active"])
    r.pieces_mlp[1] = dot_tn(r.branch[...], r.active[...]).astype(HALF)
    put(1)
    wait(get["up"])
    r.result[...] = dot_nt(r.inner[...], r.up[...])
    wait(get["middle"])

    def rows_step(image, total_gain):
        at = rows_of(cfg, image)
        unit, scale = norm(r.middle[at, :], cfg.true)
        r.normed[at, :] = (unit * r.gain_mlp[...]).astype(HALF)
        here = r.result[at, :]
        full = r.grad[at, :] + norm_back(here * r.gain_mlp[...], unit, scale, cfg.true)
        r.result[at, :] = full
        r.branch[at, :] = full.astype(HALF)
        return total_gain + jnp.sum(here * unit, axis=0, keepdims=True)

    r.gain_mlp_out[...] = lax.fori_loop(0, cfg.images, rows_step, jnp.zeros((1, width), SINGLE))
    if hasattr(r, RESULT):
        copies.put(r.result, r.result_out)
    r.pieces_mlp[0] = dot_tn(r.normed[...], r.inner[...]).astype(HALF)
    put(0)


def attention_back(cfg, r, image):
    rows, width = cfg.rows, cfg.width
    size = cfg.true // HEADS
    scale = size ** (-0.5)
    base = pl.multiple_of(image * rows, 16)
    at = pl.ds(base, rows)
    window = pl.ds(base, WINDOW)
    work = []
    for block in range(width // LANES):
        low = block * LANES
        value = r.mixed[at, 2 * width + low : 2 * width + low + LANES]
        grad_head = r.grad_heads[window, low : low + LANES]
        for head in heads_of(cfg, block)[1]:
            masked = jnp.where(lane_mask(head, size), value, jnp.zeros_like(value))
            work.append(dot_nt(masked, grad_head))
    order = 0
    for block in range(width // LANES):
        low = block * LANES
        query = r.mixed[window, low : low + LANES]
        key_t = r.mixed[at, width + low : width + low + LANES].T
        grad_head = r.grad_heads[window, low : low + LANES]
        here = heads_of(cfg, block)[1]
        grad_key = jnp.zeros((rows, LANES), SINGLE)
        grad_value = jnp.zeros((rows, LANES), SINGLE)
        parts = []
        for head in here:
            mask = lane_mask(head, size)
            grad_prob = work[order]
            order += 1
            prob = r.probs[image * HEADS + head]
            wide = prob.astype(SINGLE)
            along = jnp.sum(wide * grad_prob, axis=0, keepdims=True)
            grad_score = (wide * (grad_prob - along)).astype(HALF)
            grad_value = jnp.where(mask, dot(prob, grad_head), grad_value)
            grad_key = jnp.where(mask, dot(grad_score, query), grad_key)
            first = head * size % LANES
            parts.append(dot(key_t[first : first + size], grad_score))
        if len(here) * size < LANES:
            parts.append(jnp.zeros((LANES - len(here) * size, WINDOW), SINGLE))
        grad_query = jnp.concatenate(parts, axis=0).T[:rows]
        r.grad_mixed[at, low : low + LANES] = (grad_query * scale).astype(HALF)
        r.grad_mixed[at, width + low : width + low + LANES] = (grad_key * scale).astype(HALF)
        r.grad_mixed[at, 2 * width + low : 2 * width + low + LANES] = grad_value.astype(HALF)


def backward_attn(cfg, r, copies, get, last):
    rows, width = cfg.rows, cfg.width
    total = cfg.images * rows
    first_row = r.first_row
    if get["result"]:
        wait(get["result"])
        r.branch[...] = r.result[...].astype(HALF)
    wait(get["out"])
    r.grad_heads[0:total, :] = dot_nt(r.branch[...], r.out[...]).astype(HALF)
    r.grad_heads[total:, :] = jnp.zeros((r.grad_heads.shape[0] - total, width), HALF)

    def fill(index, value):
        value = value.astype(HALF)
        if cfg.true == width:
            r.pieces_attn[index * width : (index + 1) * width, :] = value
        else:
            pack_square(cfg, index, value, r.pieces_attn, 0)

    wait(get[HEADS_AXIS])
    fill(3, dot_tn(r.heads[...], r.branch[...]))
    wait(get["mixed"] + get["probs"])

    @pl.loop(0, cfg.images // BACKWARD_UNROLL)
    def _(step):
        for part in range(BACKWARD_UNROLL):
            attention_back(cfg, r, step * BACKWARD_UNROLL + part)

    wait(get["qkv"])
    r.grad_x[...] = dot_nt(r.grad_mixed[...], r.qkv[...])
    wait(get["x"])

    def rows_step(image, total_gain):
        at = rows_of(cfg, image)
        unit, scale = norm(r.x[at, :], cfg.true)
        r.normed[at, :] = (unit * r.gain_attn[...]).astype(HALF)
        here = r.grad_x[at, :]
        r.grad_x[at, :] = r.result[at, :] + norm_back(here * r.gain_attn[...], unit, scale, cfg.true)
        return total_gain + jnp.sum(here * unit, axis=0, keepdims=True)

    r.gain_attn_out[...] = lax.fori_loop(0, cfg.images, rows_step, jnp.zeros((1, width), SINGLE))
    if last:
        for image in range(cfg.images):
            first = image * rows
            put_tokens(cfg, r.grad_x_out, image, r.grad_x[first : first + rows, :])
    else:
        copies.put(r.grad_x, r.grad_x_out)
    for part in range(3):
        cols = slice(part * width, (part + 1) * width)
        fill(part, dot_tn(r.normed[...], r.grad_mixed[:, cols]))
    put_rows(r.place, r.pieces_attn, 0, r.keep_out, r.send_out, first_row, copies, first_row == 0)
    if hasattr(r, "lines"):
        put_lines(r, copies, first_row + r.pieces_attn.shape[0] // 8)


def backward_body(cfg, layer, attn, mlp, last, first_row, r):
    pick_layer(layer, r)
    copies = Copies(r.semaphores)
    r.first_row = first_row
    get = {"result": []}

    def begin(name):
        get[name] = [copies.begin(getattr(r, name + "_in"), getattr(r, name))]

    if mlp:
        shards = (r.own, r.core, r.far, r.both)
        begin("grad")
        get["down"] = shard_copies(cfg, copies, shards, r.down, 1)
        begin("slope")
        begin("active")
        get["up"] = shard_copies(cfg, copies, shards, r.up, 0)
        begin("middle")
    else:
        begin("result")
    if attn:
        for name in ("out", HEADS_AXIS, "mixed", "probs", "qkv", "x"):
            begin(name)
    if mlp:
        backward_mlp(cfg, r, copies, get)
    if attn:
        backward_attn(cfg, r, copies, get, last)
    copies.finish()


def put_rows(place, source, begin, keep, send, first, copies, side_first=False):
    size = (source.shape[0] - begin) // 8
    outer, inner = (1, 2) if side_first else (2, 1)
    for index in range(8):
        rows = source.at[begin + index * size : begin + (index + 1) * size]
        chunk = 2 * lax.rem(place[outer] + index // 2 % 2, 2) + lax.rem(place[inner] + index % 2, 2)
        semaphore = copies.semaphores.at[copies.block(1)]
        kept = pltpu.make_async_copy(rows, keep.at[chunk, first : first + size], semaphore)
        sent = pltpu.make_async_copy(rows, send.at[chunk, first : first + size], semaphore)
        pl.when(place[3] == index // 4)(kept.start)
        pl.when(place[3] != index // 4)(sent.start)
        copies.puts.append(kept)


def put_lines(r, copies, first):
    r.ready[...] = jnp.zeros(r.ready.shape, SINGLE)
    count = r.lines.shape[0] // 8
    own = r.gain_attn_out[...]
    for index in range(8):
        here = r.lines[index * count : (index + 1) * count, :]
        if index == 0:
            here = here + jnp.where(iota((count, 1), 0) == 0, own, 0.0)
        chunk = 2 * lax.rem(r.place[1] + index // 2 % 2, 2) + lax.rem(r.place[2] + index % 2, 2)
        other = lax.rem(r.place[3] + index // 4, 2)
        r.ready[other, chunk, 0:count, :] = here
    r.lines_half[...] = r.ready[...].astype(HALF)
    for index, target in enumerate((r.keep_out, r.send_out)):
        for chunk in range(4):
            copies.put(r.lines_half.at[index, chunk], target.at[chunk, first : first + LINE_ROWS])


def pack_square(cfg, index, piece, target, first):
    true = cfg.true
    row = first + index // 2 * true
    col = index % 2 * true
    target[row : row + true, col : col + true] = piece[0:true, 0:true]


ANY = pl.BlockSpec(memory_space=pl.ANY)
NEAR = pl.BlockSpec(memory_space=pltpu.VMEM)
SCALAR = pl.BlockSpec(memory_space=pltpu.SMEM)


def shape(dims, dtype):
    return jax.ShapeDtypeStruct(dims, dtype)


def call(name, kernel, in_specs, outs, out_specs, scratch, flops, moved):
    return pl.pallas_call(
        kernel,
        name=name,
        out_shape=outs,
        in_specs=in_specs,
        out_specs=out_specs,
        scratch_shapes=scratch,
        compiler_params=pltpu.CompilerParams(vmem_limit_bytes=VMEM_BYTES),
        cost_estimate=pl.CostEstimate(flops=flops, bytes_accessed=moved, transcendentals=0),
    )


def named_call(name, body, ins, outs, scratch, flops, aliases=()):
    names = [entry[0] for entry in ins + outs + scratch]
    positions = {entry[0]: index for index, entry in enumerate(ins)}
    places = {entry[0]: index for index, entry in enumerate(outs)}

    def kernel(*refs):
        body(types.SimpleNamespace(**dict(zip(names, refs))))

    results = pl.pallas_call(
        kernel,
        name=name,
        out_shape=[entry[1] for entry in outs],
        in_specs=[entry[2] for entry in ins],
        out_specs=[entry[2] for entry in outs],
        scratch_shapes=[entry[1] for entry in scratch],
        input_output_aliases={positions[source]: places[target] for source, target in aliases},
        compiler_params=pltpu.CompilerParams(vmem_limit_bytes=VMEM_BYTES),
        cost_estimate=pl.CostEstimate(flops=flops, bytes_accessed=10**7, transcendentals=0),
    )(*[entry[1] for entry in ins])
    return {entry[0]: result for entry, result in zip(outs, results)}


def sizes(cfg):
    total = cfg.images * cfg.rows
    return total, total + WINDOW - cfg.rows, cfg.width


def semaphores(count):
    return pltpu.SemaphoreType.DMA((count,))


def block_shapes(cfg):
    total, longer, width = sizes(cfg)
    wide = shape((total, width), SINGLE)
    narrow = shape((total, width), HALF)
    inner = shape((total, cfg.hidden), HALF)
    return {
        "x": wide,
        "middle": wide,
        "y": wide,
        "grad": wide,
        "result": wide,
        "grad_x": wide,
        "mixed": shape((longer, 3 * width), HALF),
        "probs": shape((cfg.images * HEADS, cfg.rows, WINDOW), HALF),
        HEADS_AXIS: narrow,
        "normed": narrow,
        "branch": narrow,
        "active": inner,
        "slope": inner,
        "inner": inner,
        "grad_heads": shape((longer, width), HALF),
        "grad_mixed": shape((total, 3 * width), HALF),
        "qkv": shape((width, 3 * width), HALF),
        "out": shape((width, width), HALF),
        "up": shape((width, cfg.hidden), HALF),
        "down": shape((cfg.hidden, width), HALF),
        "pieces_mlp": shape((2, width, cfg.hidden), HALF),
        "pieces_attn": shape((4 * width, width) if cfg.true == width else (2 * cfg.true, 2 * cfg.true), HALF),
        "packed": shape((4, cfg.true, 2 * cfg.true), HALF),
        "ready": shape((2, 4, LINE_ROWS, width), SINGLE),
        "lines_half": shape((2, 4, LINE_ROWS, width), HALF),
        "landing": shape(tokens_shape(cfg), HALF),
    }


def block_call(name, cfg, body, ins, outs, scratch, aliases=()):
    shapes = block_shapes(cfg)
    names = list(dict.fromkeys(scratch))
    scratch = [(entry, pltpu.VMEM(shapes[entry].shape, shapes[entry].dtype)) for entry in names]
    scratch.append(("semaphores", semaphores(56)))
    outs = [entry if len(entry) == 3 else (entry[0], shapes[entry[0][:-4]], ANY) for entry in outs]
    flops = (20 if name == "forward" else 40) * cfg.images * cfg.rows * cfg.width**2
    return named_call(name, body, ins, outs, scratch, flops, aliases)


def shard_ins(shards):
    return [(name, shard, ANY) for name, shard in zip(("own", "core", "far", "both"), shards)]


def block_forward(cfg, x, params, shards=None, place=None, middle=None):
    layer, gain_attn, qkv, out, gain_mlp = params
    attn, mlp = middle is None, shards is not None
    ins, outs, scratch = [], [], []
    if attn:
        ins += [("gain_attn", gain_attn, NEAR), ("qkv_in", qkv, ANY), ("out_in", out, ANY)]
        if place is None:
            ins.append(("x_in", x, ANY))
        else:
            ins += [("tokens", x, ANY), ("place", place, SCALAR)]
            outs.append(("x_out",))
            scratch.append("landing")
        outs += [(MIDDLE,), ("mixed_out",), ("probs_out",), ("heads_out",)]
        scratch += ["x", "qkv", "out", "mixed", "probs", HEADS_AXIS, "normed"]
    else:
        ins.append(("middle_in", middle, ANY))
    if mlp:
        ins += [("gain_mlp", gain_mlp, NEAR)] + shard_ins(shards)
        outs += [(Y_OUT,), ("active_out",), ("slope_out",)]
        scratch += ["up", "down", "active", "slope", "y"]
    scratch.append("middle")
    kept = block_call("forward", cfg, functools.partial(forward_body, cfg, layer, attn, mlp), ins, outs, scratch)
    if attn and place is None:
        kept["x_out"] = x
    if not attn:
        kept[MIDDLE] = middle
    return kept


def block_backward(cfg, place, grad, kept, params, shards, attn=True, mlp=True, last=False, lines=None):
    layer, gain_attn, qkv, out, gain_mlp = params
    packed = cfg.true != cfg.width
    ins, outs, scratch = [("place", place, SCALAR)], [], ["result", "branch", "normed"]
    rows = 0
    if mlp:
        ins += [("grad_in", grad, ANY), ("gain_mlp", gain_mlp, NEAR)] + shard_ins(shards)
        ins += [(name + "_in", kept[name + "_out"], ANY) for name in ("middle", "active", "slope")]
        outs.append((GAIN_MLP, shape((1, cfg.width), SINGLE), NEAR))
        scratch += ["grad", "middle", "active", "slope", "up", "down", "inner", "pieces_mlp"]
        scratch += ["packed"] if packed else []
        rows += cfg.true // 2 if packed else cfg.width
        if not attn:
            outs.append((RESULT,))
    first_row = rows
    if attn:
        ins += [("gain_attn", gain_attn, NEAR), ("qkv_in", qkv, ANY), ("out_in", out, ANY)]
        ins += [(name + "_in", kept[name + "_out"], ANY) for name in ("x", "mixed", "probs", HEADS_AXIS)]
        if not mlp:
            ins.append(("result_in", grad, ANY))
        outs.append((GAIN_ATTN, shape((1, cfg.width), SINGLE), NEAR))
        if last:
            outs.append((GRAD_X, shape(tokens_shape(cfg), HALF), NEAR))
        else:
            outs.append((GRAD_X,))
        rows += cfg.true // 4 if packed else cfg.width // 2
        scratch += ["x", "mixed", "probs", HEADS_AXIS, "qkv", "out", "grad_heads", "grad_mixed", "grad_x", "pieces_attn"]
        if lines is not None:
            ins.append(("lines", lines, NEAR))
            scratch += ["ready", "lines_half"]
            rows += LINE_ROWS
    chunk = shape((4, rows, 2 * cfg.true if packed else cfg.width), HALF)
    outs += [(KEEP, chunk, ANY), (SEND, chunk, ANY)]
    body = functools.partial(backward_body, cfg, layer, attn, mlp, last, first_row)
    return block_call("backward", cfg, body, ins, outs, scratch)


def class_rows(ref, cfg):
    rows = [ref[image * cfg.rows : image * cfg.rows + 1, :] for image in range(cfg.images)]
    rows.append(jnp.zeros((CLS_ROWS - cfg.images, ref.shape[1]), ref.dtype))
    return jnp.concatenate(rows, axis=0)


def pack_rows(rows, images):
    rows.append(jnp.zeros((CLS_ROWS - images, rows[0].shape[1]), rows[0].dtype))
    return jnp.concatenate(rows, axis=0)


def unite_part(
    own, other, own_ref, other_ref, own_cot, weights, grads, unit, normed, keyval, grad_keyval, grad_patch
):
    gain_in, lift, gain_attn, qkv, out, gain_back, revert = weights
    g_in, g_attn, g_back, pack = grads
    images, rows, width = other.images, other.rows, other.width
    own_small = own.true < other.true
    total = images * rows
    size = other.true // HEADS
    scale = size ** (-0.5)
    lane = iota((CLS_ROWS, width), 1)
    head_low = iota((CLS_ROWS, width), 0) * size
    head_mask = ((lane >= head_low) & (lane < head_low + size) & (lane < other.true)).astype(SINGLE)
    key_ok = iota((CLS_ROWS, WINDOW), 1) < other.length

    unit_in, scale_in = norm(class_rows(own_ref, own), own.true)
    lifted_in, slope_in = gelu_both(unit_in * gain_in[...])
    lifted_in = lifted_in.astype(HALF)
    lifted = dot(lifted_in, lift[...])
    unit_cls, scale_cls = norm(lifted, other.true)
    normed_cls = (unit_cls * gain_attn[...]).astype(HALF)

    for image in range(images):
        at = slice(image * rows, (image + 1) * rows)
        here = jnp.where(
            iota((rows, 1), 0) == 0, lifted[image : image + 1], other_ref[at, :]
        )
        unit_here, scale_here = norm(here, other.true)
        unit[at, :] = unit_here
        grad_patch[at, :] = jnp.broadcast_to(scale_here, (rows, width))
        normed[at, :] = (unit_here * gain_attn[...]).astype(HALF)

    for part in range(2):
        cols = slice(part * width, (part + 1) * width)
        keyval[0:total, cols] = dot(
            normed[...], qkv[:, (part + 1) * width : (part + 2) * width]
        ).astype(HALF)
    keyval[total:, :] = jnp.zeros((keyval.shape[0] - total, 2 * width), HALF)
    query = dot(normed_cls, qkv[:, 0:width]).astype(HALF).astype(SINGLE)
    queries, probs_all, probs_half, merged = [], [], [], []
    for image in range(images):
        window = slice(image * rows, image * rows + WINDOW)
        spread = (head_mask * query[image : image + 1]).astype(HALF)
        scores = dot_nt(spread, keyval[window, 0:width]) * scale
        scores = jnp.where(key_ok, scores, NEG)
        raised = jnp.exp(scores - jnp.max(scores, axis=1, keepdims=True))
        prob = raised / jnp.sum(raised, axis=1, keepdims=True)
        half = prob.astype(HALF)
        mixed = dot(half, keyval[window, width : 2 * width])
        merged.append(jnp.sum(mixed * head_mask, axis=0, keepdims=True))
        queries.append(spread)
        probs_all.append(prob)
        probs_half.append(half)
    merged = pack_rows(merged, images).astype(HALF)
    calibrated = lifted + dot(merged, out[...])
    unit_back, scale_back = norm(calibrated, other.true)
    back_in, slope_back = gelu_both(unit_back * gain_back[...])
    back_in = back_in.astype(HALF)
    result = dot(back_in, revert[...])

    grad_final = class_rows(own_cot, own).astype(HALF)
    g_revert = dot_tn(grad_final, back_in) if own_small else dot_tn(back_in, grad_final)
    grad_back = dot_nt(grad_final, revert[...]) * slope_back
    g_back[...] = jnp.sum(grad_back * unit_back, axis=0, keepdims=True)
    grad_cal = norm_back(grad_back * gain_back[...], unit_back, scale_back, other.true)
    grad_cross = grad_cal.astype(HALF)
    g_out = dot_tn(merged, grad_cross).astype(HALF)
    grad_merged = dot_nt(grad_cross, out[...]).astype(HALF).astype(SINGLE)
    grad_query = []
    for image in range(images):
        window = slice(image * rows, image * rows + WINDOW)
        at = slice(image * rows, (image + 1) * rows)
        spread = (head_mask * grad_merged[image : image + 1]).astype(HALF)
        grad_prob = dot_nt(spread, keyval[window, width : 2 * width])
        prob = probs_all[image]
        along = jnp.sum(prob * grad_prob, axis=1, keepdims=True)
        grad_score = (prob * (grad_prob - along)).astype(HALF)
        back = dot(grad_score, keyval[window, 0:width]) * head_mask
        grad_query.append(jnp.sum(back, axis=0, keepdims=True) * scale)
        grad_key = dot_tn(grad_score, queries[image]) * scale
        grad_value = dot_tn(probs_half[image], spread)
        grad_keyval[at, 0:width] = grad_key[:rows].astype(HALF)
        grad_keyval[at, width : 2 * width] = grad_value[:rows].astype(HALF)
    grad_query = pack_rows(grad_query, images).astype(HALF)
    g_qkv = [dot_tn(normed_cls, grad_query).astype(HALF)]
    for part in range(2):
        cols = slice(part * width, (part + 1) * width)
        g_qkv.append(dot_tn(normed[...], grad_keyval[:, cols]).astype(HALF))
    from_query = dot_nt(grad_query, qkv[:, 0:width])
    gain_total = jnp.zeros((1, width), SINGLE)
    grad_lifted = []
    for image in range(images):
        at = slice(image * rows, (image + 1) * rows)
        grad = dot_nt(grad_keyval[at, :], qkv[:, width : 3 * width])
        grad = grad + jnp.where(iota((rows, 1), 0) == 0, from_query[image : image + 1], 0.0)
        unit_here = unit[at, :]
        gain_total = gain_total + jnp.sum(grad * unit_here, axis=0, keepdims=True)
        scale_here = grad_patch[at, :]
        back = norm_back(grad * gain_attn[...], unit_here, scale_here, other.true)
        grad_patch[at, :] = back
        grad_lifted.append(back[0:1])
    g_attn[...] = gain_total
    grad_lifted = (grad_cal + pack_rows(grad_lifted, images)).astype(HALF)
    g_lift = dot_tn(lifted_in, grad_lifted) if own_small else dot_tn(grad_lifted, lifted_in)
    grad_in = dot_nt(grad_lifted, lift[...]) * slope_in
    g_in[...] = jnp.sum(grad_in * unit_in, axis=0, keepdims=True)
    grad_cls = norm_back(grad_in * gain_in[...], unit_in, scale_in, own.true)
    narrow = min(own.true, other.true)
    wide = max(own.true, other.true)
    target, row = pack
    for piece in (g_lift, g_revert):
        target[row : row + narrow, :] = piece[0:narrow, :].astype(HALF)
        row += narrow
    if own_small:
        for piece in g_qkv + [g_out]:
            target[row : row + wide, :] = piece
            row += wide
    else:
        for index, piece in enumerate(g_qkv + [g_out]):
            pack_square(other, index, piece, target, row)
    return result, grad_cls


def finish_rows(cfg, mid_ref, cot_ref, result, grad_cls, result_ref, grad_ref):
    for image in range(cfg.images):
        at = slice(image * cfg.rows, (image + 1) * cfg.rows)
        first = iota((cfg.rows, 1), 0) == 0
        rows = jnp.where(first, result[image : image + 1], mid_ref[at, :])
        put_tokens(cfg, result_ref, image, rows)
        grad_ref[at, :] = jnp.where(
            first, grad_cls[image : image + 1], grad_ref[at, :] + cot_ref[at, :]
        )


def unite_rows(small, large):
    first = 2 * small.true + 4 * large.true
    used = first + 4 * small.true
    return first, used, round_up(used, 512)


def unite_kernel(small, large, *refs):
    place, small_tokens, large_tokens, small_mid, large_mid = refs[0:5]
    first, second = refs[5:12], refs[12:19]
    small_res, large_res, grad_small, grad_large, keep, send = refs[19:25]
    first_gains, second_gains = refs[25:28], refs[28:31]
    first_work, second_work = refs[31:35], refs[35:39]
    small_land, large_land, small_cot, large_cot, packed, sems = refs[39:]
    begin, used, rows = unite_rows(small, large)
    copies = Copies(sems)
    load_tokens(small, place, small_tokens, small_land, small_cot, copies)
    load_tokens(large, place, large_tokens, large_land, large_cot, copies)
    packed[used:rows, :] = jnp.zeros((rows - used, packed.shape[1]), HALF)
    small_head, grad_small_cls = unite_part(
        small, large, small_mid, large_mid, small_cot, first, (*first_gains, (packed, 0)), *first_work, grad_large
    )
    large_head, grad_large_cls = unite_part(
        large, small, large_mid, small_mid, large_cot, second, (*second_gains, (packed, begin)), *second_work,
        grad_small,
    )
    put_rows(place, packed, 0, keep, send, 0, copies, True)
    finish_rows(small, small_mid, small_cot, small_head, grad_small_cls, small_res, grad_small)
    finish_rows(large, large_mid, large_cot, large_head, grad_large_cls, large_res, grad_large)
    copies.finish()


def unite_both(small, large, place, small_cot, large_cot, small_mid, large_mid, first, second):
    def gains(own, other):
        return [shape((1, own.width), SINGLE), shape((1, other.width), SINGLE), shape((1, other.width), SINGLE)]

    def work(other):
        total, longer, width = sizes(other)
        return [
            pltpu.VMEM((total, width), SINGLE),
            pltpu.VMEM((total, width), HALF),
            pltpu.VMEM((longer, 2 * width), HALF),
            pltpu.VMEM((total, 2 * width), HALF),
        ]

    def rows(cfg):
        return shape((cfg.images * cfg.rows, cfg.width), SINGLE)

    def tokens(cfg):
        return shape(tokens_shape(cfg), HALF)

    outs = [tokens(small), tokens(large), rows(small), rows(large)]
    packed = unite_rows(small, large)[2]
    outs += [shape((4, packed // 8, large.width), HALF)] * 2
    outs += gains(small, large) + gains(large, small)
    scratch = work(large) + work(small)
    for cfg in (small, large):
        scratch.append(pltpu.VMEM(tokens_shape(cfg), HALF))
    for cfg in (small, large):
        scratch.append(pltpu.VMEM((cfg.images * cfg.rows, cfg.width), SINGLE))
    scratch += [pltpu.VMEM((packed, large.width), HALF), semaphores(10)]
    return call(
        "unite", functools.partial(unite_kernel, small, large), [SCALAR, ANY, ANY] + [NEAR] * 16, outs,
        [NEAR] * 4 + [ANY] * 2 + [NEAR] * 6, scratch, 30 * large.images * large.rows * large.width**2, 10**7,
    )(place, small_cot, large_cot, small_mid, large_mid, *first, *second)


def pad_dims(array, dims):
    return jnp.pad(array, [(0, dim - old) for old, dim in zip(array.shape, dims)])


def prepare_kernel(small, large, *refs):
    ins, outs, up, down, sems = refs[0:20], refs[20:-3], refs[-3], refs[-2], refs[-1]
    stacked = outs[17:]
    copies = Copies(sems)
    gets = []
    for layer in range(len(stacked)):
        gets.append(copies.begin(ins[18].at[layer], up.at[layer]))
        gets.append(copies.begin(ins[19].at[layer], down.at[layer]))
    for layer, target in enumerate(stacked):
        gets[2 * layer].wait()
        copies.put(up.at[layer], target.at[0])
        gets[2 * layer + 1].wait()
        copies.put(down.at[layer], target.at[1])
    shard = outs[16]
    shard[...] = jnp.zeros(shard.shape, HALF)
    for index in range(2):
        matrix = ins[16 + index]
        shard[index, 0 : matrix.shape[0], 0 : matrix.shape[1]] = matrix[...]
    for source, target in zip(ins[0:16], outs[0:16]):
        tall, wide = source.shape
        target[...] = jnp.zeros(target.shape, target.dtype)
        if wide == 3 * small.true and tall == small.true:
            for part in range(3):
                cols = slice(part * small.width, part * small.width + tall)
                target[0:tall, cols] = source[:, part * tall : (part + 1) * tall]
        elif tall == small.true and target.shape[0] == large.width:
            target[0:wide, 0:tall] = source[...].astype(SINGLE).T.astype(target.dtype)
        else:
            target[0:tall, 0:wide] = source[...]
    copies.finish()


def prepare(small, large, small_params, first, second, large_up, large_down):
    gain_attn, qkv, out, gain_mlp, up, down = small_params
    depth = large_up.shape[0]
    ns, nl = small.width, large.width
    squares = [gain_attn[None], qkv, out, gain_mlp[None]]
    sizes_out = [(1, ns), (ns, 3 * ns), (ns, ns), (1, ns)]

    def unite_pads(weights, own, other):
        gain_in, lift, gain, qkv, out, gain_back, revert = weights
        lift, revert = [matrix.T if matrix.shape[0] > matrix.shape[1] else matrix for matrix in (lift, revert)]
        arrays = [gain_in[None], lift, gain[None], out, gain_back[None], revert]
        shapes = [(1, own), (own, other), (1, other), (other, other), (1, other), (other, own)]
        return arrays, shapes, qkv, (other, 3 * other)

    first_arrays, first_shapes, first_qkv, _ = unite_pads(first, ns, nl)
    second_arrays, second_shapes, second_qkv, second_dims = unite_pads(second, nl, ns)
    need = [0, 1, 5]
    arrays = squares + [first_arrays[index] for index in need] + second_arrays + [second_qkv]
    dims = sizes_out + [first_shapes[index] for index in need] + second_shapes + [second_dims]
    extra = 16 - len(arrays)
    arrays += [gain_attn[None]] * extra
    dims += [(1, ns)] * extra
    outs = [shape(size, array.dtype) for size, array in zip(dims, arrays)]
    outs += [shape((2, ns, small.hidden // 4), HALF)]
    outs += [shape((2, nl, nl), HALF)] * depth
    results = call(
        "prepare", functools.partial(prepare_kernel, small, large), [NEAR] * 18 + [ANY] * 2, outs,
        [NEAR] * 17 + [ANY] * depth,
        [pltpu.VMEM(large_up.shape, HALF), pltpu.VMEM(large_down.shape, HALF), semaphores(4 * depth)], 10**6, 10**7,
    )(*arrays, up, down, large_up, large_down)
    small_ready = results[0:4]
    f_in, f_lift, f_revert = results[4:7]
    s_in, s_lift, s_attn, s_out, s_back, s_revert, s_qkv = results[7:14]
    first_ready = (f_in, f_lift, first_arrays[2], first_qkv, first_arrays[3], first_arrays[4], f_revert)
    second_ready = (s_in, s_lift, s_attn, s_qkv, s_out, s_back, s_revert)
    return small_ready, first_ready, second_ready, results[16], results[17:]


def plus(*terms):
    total = terms[0].astype(SINGLE)
    for term in terms[1:]:
        total = total + term.astype(SINGLE)
    return total.astype(HALF)


class Links:
    def __init__(self):
        heads, dp = lax.axis_size(HEADS_AXIS), lax.axis_size(ROW_AXIS)
        place, row = lax.axis_index(HEADS_AXIS), lax.axis_index(ROW_AXIS)
        self.heads, self.dp = heads, dp
        self.core, self.far, self.side = place % 2, place // 2, row % 2

    def scalars(self):
        place = lax.axis_index(HEADS_AXIS)
        return jnp.stack([place, self.side, self.far, self.core]).astype(jnp.int32)

    def swap(self, array, axis, bit):
        size = self.heads if axis == HEADS_AXIS else self.dp
        return lax.ppermute(array, axis, [(index, index ^ bit) for index in range(size)])

    def by_core(self, array):
        return self.swap(array, HEADS_AXIS, 1)

    def by_far(self, array):
        return self.swap(array, HEADS_AXIS, 2)

    def by_side(self, array):
        return self.swap(array, ROW_AXIS, 1)

    def long_steps(self):
        bits = [2 << step for step in range((self.dp // 2).bit_length() - 1)]
        if len(bits) == 2:
            bits = [2, 6]
        return [functools.partial(self.swap, axis=ROW_AXIS, bit=bit) for bit in bits]


def whole(mine, other, index):
    return jnp.where(index == 0, jnp.stack([mine, other]), jnp.stack([other, mine]))


def reduce_steps(links, keep, send, shared):
    owned = keep.shape[1] - shared
    lanes = keep.shape[2]
    outer, inner = (links.by_far, links.far), (links.by_side, links.side)
    if not owned:
        outer, inner = inner, outer
    (send,) = yield [send]
    got = links.by_core(send)
    away, own = yield [plus(keep[2:4], got[2:4]), plus(keep[0:2], got[0:2])]
    got = outer[0](away)
    away, own = yield [plus(own[1], got[1]), plus(own[0], got[0])]
    (own,) = yield [plus(own, inner[0](away))]
    for step in links.long_steps():
        (own,) = yield [plus(own, step(own))]
    got = inner[0](own)
    hidden = whole(own[:owned], got[:owned], inner[1]) if owned else None
    if not shared:
        return hidden, None
    (mine,) = yield [whole(own[owned:], got[owned:], inner[1]).reshape(-1, lanes)]
    (mine,) = yield [whole(mine, outer[0](mine), outer[1]).reshape(-1, lanes)]
    return hidden, whole(mine, links.by_core(mine), links.core).reshape(-1, lanes)


class Rounds:
    def __init__(self):
        self.active = {}
        self.waiting = {}
        self.done = {}

    def add(self, name, steps):
        self.active[name] = steps
        self.waiting[name] = next(steps)

    def tie(self, names, *arrays):
        names = [name for name in (self.active if names is None else names) if name in self.active]
        held = {name: self.waiting[name] for name in names}
        if held:
            arrays, held = lax.optimization_barrier((arrays, held))
        for name in names:
            try:
                self.waiting[name] = self.active[name].send(held[name])
            except StopIteration as stop:
                self.done[name] = stop.value
                del self.active[name], self.waiting[name]
        return arrays if len(arrays) != 1 else arrays[0]


def per_device(
    small_tokens,
    large_tokens,
    small_cotangent,
    large_cotangent,
    small_gain_attn,
    small_qkv,
    small_out,
    small_gain_mlp,
    small_up,
    small_down,
    large_gain_attn,
    large_qkv,
    large_out,
    large_gain_mlp,
    large_up,
    large_down,
    *unite_weights,
):
    devices = lax.axis_size(HEADS_AXIS)
    depth = large_qkv.shape[0]
    images = small_tokens.shape[0] // devices
    links = Links()
    place = links.scalars()

    def branch(tokens, hidden):
        _, length, true = tokens.shape
        return Branch(images, round_up(length, 16), length, round_up(true, LANES), true, hidden * devices)

    small = branch(small_tokens, round_up(small_up.shape[1], LANES))
    large = branch(large_tokens, large_up.shape[2])
    small_ready, first, second, small_shard, large_shards = prepare(
        small,
        large,
        (small_gain_attn, small_qkv, small_out, small_gain_mlp, small_up, small_down),
        unite_weights[0:7],
        unite_weights[7:14],
        large_up,
        large_down,
    )

    def after(value, *others):
        return lax.optimization_barrier((value, *others))[0]

    def spread(shard, far):
        return (shard, links.by_core(shard), far, links.by_core(far))

    far_small = links.by_far(small_shard)
    far = [links.by_far(large_shards[0])]
    large_gains = [(large_gain_attn[layer][None], large_gain_mlp[layer][None]) for layer in range(depth)]

    small_block = (None, *small_ready[0:4])
    large_blocks = [
        (layer, large_gains[layer][0], large_qkv, large_out, large_gains[layer][1]) for layer in range(depth)
    ]
    small_tokens, small_cotangent = small_tokens.swapaxes(1, 2), small_cotangent.swapaxes(1, 2)
    small_kept = block_forward(small, small_tokens, small_block, None, place)
    tokens, small_kept[MIDDLE] = lax.optimization_barrier((large_tokens, small_kept[MIDDLE]))
    large_kept, large_weights = [], []
    kept = block_forward(large, tokens, large_blocks[0], None, place)
    small_middle, middle, far[0], far_small = lax.optimization_barrier(
        (small_kept[MIDDLE], kept[MIDDLE], far[0], far_small)
    )
    small_weights = spread(small_shard, far_small)
    large_weights.append(spread(large_shards[0], far[0]))
    far.append(links.by_far(after(large_shards[1], far[0])))
    small_kept |= block_forward(small, None, small_block, small_weights, None, small_middle)
    middle = after(middle, small_kept[Y_OUT])
    kept |= block_forward(large, None, large_blocks[0], large_weights[0], None, middle)
    large_kept.append(kept)
    state = kept[Y_OUT]
    for layer in range(1, depth):
        state, far[layer] = lax.optimization_barrier((state, far[layer]))
        large_weights.append(spread(large_shards[layer], far[layer]))
        if layer + 1 < depth:
            far.append(links.by_far(after(large_shards[layer + 1], far[layer])))
        large_kept.append(block_forward(large, state, large_blocks[layer], large_weights[layer]))
        state = large_kept[layer][Y_OUT]
    small_mid = small_kept[Y_OUT]

    small_res, large_res, grad_small, grad, keep, send, *unite_gains = unite_both(
        small, large, place, small_cotangent, large_cotangent, small_mid, state, first, second
    )

    def gather(array):
        return lax.all_gather(array, HEADS_AXIS, axis=0, tiled=True)

    small_result, large_result = gather(small_res).swapaxes(1, 2), gather(large_res)
    rounds = Rounds()
    rounds.add("unite", reduce_steps(links, keep, send, keep.shape[1]))
    gains = [None] * depth
    lanes = large.width

    def large_back(layer):
        back = block_backward(large, place, rounds.tie(None, grad), large_kept[layer], large_blocks[layer], large_weights[layer])
        gains[layer] = (back[GAIN_ATTN], back[GAIN_MLP])
        rounds.add("large%d" % layer, reduce_steps(links, back[KEEP], back[SEND], lanes // 2))
        return back[GRAD_X]

    for layer in range(depth - 1, 0, -1):
        if layer == 1:
            grad, grad_small = lax.optimization_barrier((grad, grad_small))
            grad_small = rounds.tie(None, grad_small)
            back = block_backward(small, place, grad_small, small_kept, small_block, small_weights, last=True)
            rounds.add("small", reduce_steps(links, back[KEEP], back[SEND], small.true // 4))
            small_grad = gather(back[GRAD_X]).swapaxes(1, 2).astype(SINGLE)
            small_gains = [back[GAIN_ATTN], back[GAIN_MLP]]
            grad, small_gains = lax.optimization_barrier((grad, small_gains))
        grad = large_back(layer)
    grad = rounds.tie(None, grad)
    back = block_backward(large, place, grad, large_kept[0], large_blocks[0], large_weights[0], attn=False)
    rounds.add("hidden0", reduce_steps(links, back[KEEP], back[SEND], 0))
    gains[0] = (jnp.zeros((1, lanes), SINGLE), back[GAIN_MLP])
    lines = [gain for pair in gains for gain in pair] + small_gains + unite_gains
    lines = jnp.concatenate([pad_dims(line, (1, lanes)) for line in lines])
    lines = pad_dims(lines, (round_up(lines.shape[0], 8), lanes))
    grad = rounds.tie(None, back[RESULT])
    back = block_backward(
        large, place, grad, large_kept[0], large_blocks[0], None, mlp=False, last=True, lines=lines
    )
    rounds.add("large0", reduce_steps(links, back[KEEP], back[SEND], lanes // 2 + LINE_ROWS))
    large_grad = gather(back[GRAD_X]).astype(SINGLE)
    while rounds.active:
        rounds.tie(None)

    true = small.true

    def square(rows):
        (q, k), (v, o) = [jnp.split(half, 2, axis=1) for half in jnp.split(rows, 2, axis=0)]
        return jnp.concatenate([q, k, v], axis=1), o

    def full(rows):
        q, k, v, o = jnp.split(rows, 4, axis=0)
        return jnp.concatenate([q, k, v], axis=1), o

    s_hidden, s_rest = rounds.done["small"]
    s_hidden = s_hidden.reshape(true, 2 * true).astype(SINGLE)
    s_qkv, s_out = square(s_rest.astype(SINGLE))
    count = lines.shape[0] // 8
    last = rounds.done["large0"][1].reshape(8, -1, lanes)
    line = last[:, lanes // 2 : lanes // 2 + count].reshape(8 * count, lanes).astype(SINGLE)
    first_rest = last[:, : lanes // 2].reshape(4 * lanes, lanes)
    at = 2 * depth
    l_hidden = [rounds.done["large%d" % layer if layer else "hidden0"][0] for layer in range(depth)]
    l_rest = [full(rounds.done["large%d" % layer][1] if layer else first_rest) for layer in range(depth)]
    u_rest = rounds.done["unite"][1].astype(SINGLE)
    begin, used, _ = unite_rows(small, large)
    f_qkv, f_out = full(u_rest[2 * true : begin])
    u_second = u_rest[begin:used]
    e_qkv, e_out = square(u_second[2 * true :])
    return (
        small_result,
        large_result,
        small_grad,
        large_grad,
        line[at, :true],
        s_qkv,
        s_out,
        line[at + 1, :true],
        s_hidden[:, :true],
        s_hidden[:, true:].T,
        line[0:at:2],
        jnp.stack([pair[0] for pair in l_rest]).astype(SINGLE),
        jnp.stack([pair[1] for pair in l_rest]).astype(SINGLE),
        line[1:at:2],
        jnp.stack([pair[0] for pair in l_hidden]).astype(SINGLE),
        jnp.stack([pair[1] for pair in l_hidden]).swapaxes(1, 2).astype(SINGLE),
        line[at + 2, :true],
        u_rest[:true],
        line[at + 3],
        f_qkv,
        f_out,
        line[at + 4],
        u_rest[true : 2 * true].T,
        line[at + 5],
        u_second[:true].T,
        line[at + 6, :true],
        e_qkv,
        e_out,
        line[at + 7, :true],
        u_second[true : 2 * true],
    )


def solution(mesh):
    rows = P(ROW_AXIS, None, None)
    copied = P()
    split = [copied] * 4 + [P(None, HEADS_AXIS), P(HEADS_AXIS, None)]
    stack = [copied] * 4 + [P(None, None, HEADS_AXIS), P(None, HEADS_AXIS, None)]
    specs = tuple([rows] * 4 + split + stack + [copied] * 14)
    return jax.shard_map(per_device, mesh=mesh, in_specs=specs, out_specs=specs, check_vma=False)
```

```python
import collections
import functools
import types

import jax
import jax.numpy as jnp
from jax import lax
from jax.experimental import pallas as pl
from jax.experimental.pallas import tpu as pltpu
from jax.sharding import PartitionSpec as P

HEADS_AXIS, ROW_AXIS = "heads", "dp"
MIDDLE, RESULT, Y_OUT, GRAD_X = "middle_out", "result_out", "y_out", "grad_x_out"
KEEP, SEND, GAIN_ATTN, GAIN_MLP = "keep_out", "send_out", "gain_attn_out", "gain_mlp_out"
EPS = 1e-06
SINGLE = jnp.float32
HALF = jnp.bfloat16
HEADS = 6
LANES = 128
WINDOW = 256
CLS_ROWS = 16
NEG = -1e30
ROOT_HALF = 0.7071067811865476
INV_ROOT_2PI = 0.3989422804014327
VMEM_BYTES = 60 * 1024 * 1024
FORWARD_UNROLL = 4
LINE_ROWS = 16
BACKWARD_UNROLL = 4

Branch = collections.namedtuple("Branch", ("images", "rows", "length", "width", "true", "hidden"))


def round_up(value, step):
    return -(-value // step) * step


def dot(left, right):
    return jnp.dot(left, right, preferred_element_type=SINGLE)


def dot_nt(left, right):
    return lax.dot_general(left, right, (((1,), (1,)), ((), ())), preferred_element_type=SINGLE)


def dot_tn(left, right):
    return lax.dot_general(left, right, (((0,), (0,)), ((), ())), preferred_element_type=SINGLE)


def iota(shape, dim):
    return lax.broadcasted_iota(jnp.int32, shape, dim)


def norm(values, true):
    width = values.shape[-1]
    mean = jnp.sum(values, axis=-1, keepdims=True) * (1.0 / true)
    center = values - mean
    if true != width:
        center = jnp.where(iota((1, width), 1) < true, center, 0.0)
    spread = jnp.sum(center * center, axis=-1, keepdims=True) * (1.0 / true)
    scale = lax.rsqrt(spread + EPS)
    return center * scale, scale


def norm_back(grad, unit, scale, true):
    mean = jnp.sum(grad, axis=-1, keepdims=True) * (1.0 / true)
    along = jnp.sum(grad * unit, axis=-1, keepdims=True) * (1.0 / true)
    return scale * (grad - mean - unit * along)


def gelu_both(values):
    phi = 0.5 + 0.5 * lax.erf(values * ROOT_HALF)
    density = jnp.exp(values * values * -0.5) * INV_ROOT_2PI
    return values * phi, phi + values * density


def heads_of(cfg, block):
    size = cfg.true // HEADS
    per = LANES // size
    first = block * per
    return size, [head for head in range(first, min(first + per, HEADS))]


def lane_mask(head, size):
    low = head * size % LANES
    lane = iota((1, LANES), 1)
    return (lane >= low) & (lane < low + size)


class Copies:
    def __init__(self, semaphores):
        self.semaphores, self.used, self.puts = semaphores, 0, []

    def begin(self, source, target):
        copy = pltpu.make_async_copy(source, target, self.semaphores.at[self.used])
        self.used += 1
        copy.start()
        return copy

    def put(self, source, target):
        self.puts.append(self.begin(source, target))

    def block(self, count):
        self.used += count
        return self.used - count

    def finish(self):
        for copy in self.puts:
            copy.wait()


def wait(copies):
    for copy in copies:
        copy.wait()


def flipped(cfg):
    return cfg.true != cfg.width


def tokens_shape(cfg):
    return (cfg.images, cfg.true, cfg.length) if flipped(cfg) else (cfg.images, cfg.length, cfg.true)


def put_tokens(cfg, target, image, rows):
    rows = rows.T if flipped(cfg) else rows
    target[image] = rows[0 : target.shape[1], 0 : target.shape[2]].astype(HALF)


def load_tokens(cfg, place, tokens, landing, target, copies):
    copy = copies.begin(tokens.at[pl.ds(place[0] * cfg.images, cfg.images)], landing)
    target[...] = jnp.zeros(target.shape, target.dtype)
    copy.wait()
    for image in range(cfg.images):
        first = image * cfg.rows
        rows = landing[image].astype(target.dtype)
        target[first : first + cfg.length, 0 : cfg.true] = rows.T if flipped(cfg) else rows


def shard_copies(cfg, copies, shards, target, index):
    size = cfg.hidden // 4
    gets = []
    for number, shard in enumerate(shards):
        part = slice(number * size, (number + 1) * size)
        gets.append(copies.begin(shard.at[index], target.at[:, part] if index == 0 else target.at[part, :]))
    return gets


def rows_of(cfg, image):
    return pl.ds(pl.multiple_of(image * cfg.rows, 16), cfg.rows)


def attention(cfg, mixed, heads, probs, image, key_ok, query_ok):
    rows, width = cfg.rows, cfg.width
    work = []
    for block in range(width // LANES):
        low = block * LANES
        base = pl.multiple_of(image * rows, 16)
        query = mixed[pl.ds(base, WINDOW), low : low + LANES]
        key = mixed[pl.ds(base, rows), width + low : width + low + LANES]
        size, here = heads_of(cfg, block)
        for head in here:
            masked = jnp.where(lane_mask(head, size), key, jnp.zeros_like(key))
            work.append(dot_nt(masked, query))
    order = 0
    for block in range(width // LANES):
        low = block * LANES
        base = pl.multiple_of(image * rows, 16)
        value_t = mixed[pl.ds(base, rows), 2 * width + low : 2 * width + low + LANES].T
        size, here = heads_of(cfg, block)
        pieces = []
        for head in here:
            scores = jnp.where(key_ok, work[order] * size ** (-0.5), NEG)
            order += 1
            top = jnp.max(scores, axis=0, keepdims=True)
            raised = jnp.exp(scores - top)
            total_row = jnp.sum(raised, axis=0, keepdims=True)
            prob = (raised * (query_ok / total_row)).astype(HALF)
            probs[image * HEADS + head] = prob
            first = head * size % LANES
            pieces.append(dot(value_t[first : first + size], prob))
        if len(here) * size < LANES:
            pieces.append(jnp.zeros((LANES - len(here) * size, WINDOW), SINGLE))
        heads[pl.ds(base, rows), low : low + LANES] = jnp.concatenate(pieces, axis=0).T[:rows].astype(HALF)


def forward_attn(cfg, r, copies, get_x, get_qkv, get_out):
    rows, width = cfg.rows, cfg.width
    total = cfg.images * rows
    wait(get_x)

    @pl.loop(0, cfg.images)
    def _(image):
        at = rows_of(cfg, image)
        unit, _ = norm(r.x[at, :], cfg.true)
        r.normed[at, :] = (unit * r.gain_attn[...]).astype(HALF)

    wait(get_qkv)
    for part in range(3):
        cols = slice(part * width, (part + 1) * width)
        r.mixed[0:total, cols] = dot(r.normed[...], r.qkv[:, cols]).astype(HALF)
    r.mixed[total:, :] = jnp.zeros((r.mixed.shape[0] - total, 3 * width), HALF)
    copies.put(r.mixed, r.mixed_out)

    key_ok = iota((rows, WINDOW), 0) < cfg.length
    query_ok = (iota((1, WINDOW), 1) < cfg.length).astype(SINGLE)

    @pl.loop(0, cfg.images // FORWARD_UNROLL)
    def _(step):
        for part in range(FORWARD_UNROLL):
            attention(cfg, r.mixed, r.heads, r.probs, step * FORWARD_UNROLL + part, key_ok, query_ok)

    copies.put(r.probs, r.probs_out)
    copies.put(r.heads, r.heads_out)
    wait(get_out)
    r.middle[...] = r.x[...] + dot(r.heads[...], r.out[...])
    copies.put(r.middle, r.middle_out)


def forward_mlp(cfg, r, copies, get_middle, get_up, get_down):
    first = copies.block(2 * cfg.images)
    wait(get_middle + get_up)

    def puts(image):
        at = rows_of(cfg, image)
        return [
            pltpu.make_async_copy(r.active.at[at], r.active_out.at[at], copies.semaphores.at[first + 2 * image]),
            pltpu.make_async_copy(r.slope.at[at], r.slope_out.at[at], copies.semaphores.at[first + 2 * image + 1]),
        ]

    @pl.loop(0, cfg.images)
    def _(image):
        at = rows_of(cfg, image)
        unit, _ = norm(r.middle[at, :], cfg.true)
        normed = (unit * r.gain_mlp[...]).astype(HALF)
        for low in range(0, cfg.hidden, WINDOW):
            cols = slice(low, low + WINDOW)
            act, grad = gelu_both(dot(normed, r.up[:, cols]))
            r.active[at, cols] = act.astype(HALF)
            r.slope[at, cols] = grad.astype(HALF)
        for copy in puts(image):
            copy.start()

    wait(get_down)
    half = cfg.images * cfg.rows // 2
    for part in range(2):
        at = slice(part * half, (part + 1) * half)
        r.y[at, :] = r.middle[at, :] + dot(r.active[at, :], r.down[...])
        copies.put(r.y.at[at], r.y_out.at[at])
    for image in range(cfg.images):
        wait(puts(image))


def pick_layer(layer, r):
    if layer is not None and hasattr(r, "qkv_in"):
        r.qkv_in, r.out_in = r.qkv_in.at[layer], r.out_in.at[layer]


def forward_body(cfg, layer, attn, mlp, r):
    pick_layer(layer, r)
    copies = Copies(r.semaphores)
    get_x = get_middle = get_up = get_down = []
    if attn:
        if hasattr(r, "tokens"):
            load_tokens(cfg, r.place, r.tokens, r.landing, r.x, copies)
            copies.put(r.x, r.x_out)
        else:
            get_x = [copies.begin(r.x_in, r.x)]
        get_qkv = [copies.begin(r.qkv_in, r.qkv)]
        get_out = [copies.begin(r.out_in, r.out)]
    else:
        get_middle = [copies.begin(r.middle_in, r.middle)]
    if mlp:
        shards = (r.own, r.core, r.far, r.both)
        get_up = shard_copies(cfg, copies, shards, r.up, 0)
        get_down = shard_copies(cfg, copies, shards, r.down, 1)
    if attn:
        forward_attn(cfg, r, copies, get_x, get_qkv, get_out)
    if mlp:
        forward_mlp(cfg, r, copies, get_middle, get_up, get_down)
    copies.finish()


def backward_mlp(cfg, r, copies, get):
    rows, width = cfg.rows, cfg.width
    size = cfg.hidden // 4
    wait(get["grad"])
    r.branch[...] = r.grad[...].astype(HALF)
    wait(get["down"] + get["slope"])

    @pl.loop(0, cfg.images)
    def _(image):
        at = rows_of(cfg, image)
        for low in range(0, cfg.hidden, WINDOW):
            cols = slice(low, low + WINDOW)
            grad_active = dot_nt(r.branch[at, :], r.down[cols, :])
            r.inner[at, cols] = (grad_active * r.slope[at, cols].astype(SINGLE)).astype(HALF)

    def put(index):
        for shard in range(4):
            target = (r.keep_out, r.send_out)[shard % 2]
            cols = slice(shard * size, (shard + 1) * size)
            if cfg.true == width:
                chunk = target.at[shard // 2 * 2 + lax.rem(r.place[1] + index, 2), 0:width]
                copies.put(r.pieces_mlp.at[index, :, cols], chunk)
            else:
                at = slice(index * cfg.true, (index + 1) * cfg.true)
                r.packed[shard, :, at] = r.pieces_mlp[index, 0 : cfg.true, cols][:, 0 : cfg.true]
                if index == 0:
                    half = cfg.true // 2
                    for side in range(2):
                        chunk = shard // 2 * 2 + lax.rem(r.place[1] + side, 2)
                        rows_here = slice(side * half, (side + 1) * half)
                        copies.put(r.packed.at[shard, rows_here], target.at[chunk, 0:half])

    wait(get["active"])
    r.pieces_mlp[1] = dot_tn(r.branch[...], r.active[...]).astype(HALF)
    put(1)
    wait(get["up"])
    r.result[...] = dot_nt(r.inner[...], r.up[...])
    wait(get["middle"])

    def rows_step(image, total_gain):
        at = rows_of(cfg, image)
        unit, scale = norm(r.middle[at, :], cfg.true)
        r.normed[at, :] = (unit * r.gain_mlp[...]).astype(HALF)
        here = r.result[at, :]
        full = r.grad[at, :] + norm_back(here * r.gain_mlp[...], unit, scale, cfg.true)
        r.result[at, :] = full
        r.branch[at, :] = full.astype(HALF)
        return total_gain + jnp.sum(here * unit, axis=0, keepdims=True)

    r.gain_mlp_out[...] = lax.fori_loop(0, cfg.images, rows_step, jnp.zeros((1, width), SINGLE))
    if hasattr(r, RESULT):
        copies.put(r.result, r.result_out)
    r.pieces_mlp[0] = dot_tn(r.normed[...], r.inner[...]).astype(HALF)
    put(0)


def attention_back(cfg, r, image):
    rows, width = cfg.rows, cfg.width
    size = cfg.true // HEADS
    scale = size ** (-0.5)
    base = pl.multiple_of(image * rows, 16)
    at = pl.ds(base, rows)
    window = pl.ds(base, WINDOW)
    work = []
    for block in range(width // LANES):
        low = block * LANES
        value = r.mixed[at, 2 * width + low : 2 * width + low + LANES]
        grad_head = r.grad_heads[window, low : low + LANES]
        for head in heads_of(cfg, block)[1]:
            masked = jnp.where(lane_mask(head, size), value, jnp.zeros_like(value))
            work.append(dot_nt(masked, grad_head))
    order = 0
    for block in range(width // LANES):
        low = block * LANES
        query = r.mixed[window, low : low + LANES]
        key_t = r.mixed[at, width + low : width + low + LANES].T
        grad_head = r.grad_heads[window, low : low + LANES]
        here = heads_of(cfg, block)[1]
        grad_key = jnp.zeros((rows, LANES), SINGLE)
        grad_value = jnp.zeros((rows, LANES), SINGLE)
        parts = []
        for head in here:
            mask = lane_mask(head, size)
            grad_prob = work[order]
            order += 1
            prob = r.probs[image * HEADS + head]
            wide = prob.astype(SINGLE)
            along = jnp.sum(wide * grad_prob, axis=0, keepdims=True)
            grad_score = (wide * (grad_prob - along)).astype(HALF)
            grad_value = jnp.where(mask, dot(prob, grad_head), grad_value)
            grad_key = jnp.where(mask, dot(grad_score, query), grad_key)
            first = head * size % LANES
            parts.append(dot(key_t[first : first + size], grad_score))
        if len(here) * size < LANES:
            parts.append(jnp.zeros((LANES - len(here) * size, WINDOW), SINGLE))
        grad_query = jnp.concatenate(parts, axis=0).T[:rows]
        r.grad_mixed[at, low : low + LANES] = (grad_query * scale).astype(HALF)
        r.grad_mixed[at, width + low : width + low + LANES] = (grad_key * scale).astype(HALF)
        r.grad_mixed[at, 2 * width + low : 2 * width + low + LANES] = grad_value.astype(HALF)


def backward_attn(cfg, r, copies, get, last):
    rows, width = cfg.rows, cfg.width
    total = cfg.images * rows
    first_row = r.first_row
    if get["result"]:
        wait(get["result"])
        r.branch[...] = r.result[...].astype(HALF)
    wait(get["out"])
    r.grad_heads[0:total, :] = dot_nt(r.branch[...], r.out[...]).astype(HALF)
    r.grad_heads[total:, :] = jnp.zeros((r.grad_heads.shape[0] - total, width), HALF)

    def fill(index, value):
        value = value.astype(HALF)
        if cfg.true == width:
            r.pieces_attn[index * width : (index + 1) * width, :] = value
        else:
            pack_square(cfg, index, value, r.pieces_attn, 0)

    wait(get[HEADS_AXIS])
    fill(3, dot_tn(r.heads[...], r.branch[...]))
    wait(get["mixed"] + get["probs"])

    @pl.loop(0, cfg.images // BACKWARD_UNROLL)
    def _(step):
        for part in range(BACKWARD_UNROLL):
            attention_back(cfg, r, step * BACKWARD_UNROLL + part)

    wait(get["qkv"])
    r.grad_x[...] = dot_nt(r.grad_mixed[...], r.qkv[...])
    wait(get["x"])

    def rows_step(image, total_gain):
        at = rows_of(cfg, image)
        unit, scale = norm(r.x[at, :], cfg.true)
        r.normed[at, :] = (unit * r.gain_attn[...]).astype(HALF)
        here = r.grad_x[at, :]
        r.grad_x[at, :] = r.result[at, :] + norm_back(here * r.gain_attn[...], unit, scale, cfg.true)
        return total_gain + jnp.sum(here * unit, axis=0, keepdims=True)

    r.gain_attn_out[...] = lax.fori_loop(0, cfg.images, rows_step, jnp.zeros((1, width), SINGLE))
    if last:
        for image in range(cfg.images):
            first = image * rows
            put_tokens(cfg, r.grad_x_out, image, r.grad_x[first : first + rows, :])
    else:
        copies.put(r.grad_x, r.grad_x_out)
    for part in range(3):
        cols = slice(part * width, (part + 1) * width)
        fill(part, dot_tn(r.normed[...], r.grad_mixed[:, cols]))
    put_rows(r.place, r.pieces_attn, 0, r.keep_out, r.send_out, first_row, copies, first_row == 0)
    if hasattr(r, "lines"):
        put_lines(r, copies, first_row + r.pieces_attn.shape[0] // 8)


def backward_body(cfg, layer, attn, mlp, last, first_row, r):
    pick_layer(layer, r)
    copies = Copies(r.semaphores)
    r.first_row = first_row
    get = {"result": []}

    def begin(name):
        get[name] = [copies.begin(getattr(r, name + "_in"), getattr(r, name))]

    if mlp:
        shards = (r.own, r.core, r.far, r.both)
        begin("grad")
        get["down"] = shard_copies(cfg, copies, shards, r.down, 1)
        begin("slope")
        begin("active")
        get["up"] = shard_copies(cfg, copies, shards, r.up, 0)
        begin("middle")
    else:
        begin("result")
    if attn:
        for name in ("out", HEADS_AXIS, "mixed", "probs", "qkv", "x"):
            begin(name)
    if mlp:
        backward_mlp(cfg, r, copies, get)
    if attn:
        backward_attn(cfg, r, copies, get, last)
    copies.finish()


def put_rows(place, source, begin, keep, send, first, copies, side_first=False):
    size = (source.shape[0] - begin) // 8
    outer, inner = (1, 2) if side_first else (2, 1)
    for index in range(8):
        rows = source.at[begin + index * size : begin + (index + 1) * size]
        chunk = 2 * lax.rem(place[outer] + index // 2 % 2, 2) + lax.rem(place[inner] + index % 2, 2)
        semaphore = copies.semaphores.at[copies.block(1)]
        kept = pltpu.make_async_copy(rows, keep.at[chunk, first : first + size], semaphore)
        sent = pltpu.make_async_copy(rows, send.at[chunk, first : first + size], semaphore)
        pl.when(place[3] == index // 4)(kept.start)
        pl.when(place[3] != index // 4)(sent.start)
        copies.puts.append(kept)


def put_lines(r, copies, first):
    r.ready[...] = jnp.zeros(r.ready.shape, SINGLE)
    count = r.lines.shape[0] // 8
    own = r.gain_attn_out[...]
    for index in range(8):
        here = r.lines[index * count : (index + 1) * count, :]
        if index == 0:
            here = here + jnp.where(iota((count, 1), 0) == 0, own, 0.0)
        chunk = 2 * lax.rem(r.place[1] + index // 2 % 2, 2) + lax.rem(r.place[2] + index % 2, 2)
        other = lax.rem(r.place[3] + index // 4, 2)
        r.ready[other, chunk, 0:count, :] = here
    r.lines_half[...] = r.ready[...].astype(HALF)
    for index, target in enumerate((r.keep_out, r.send_out)):
        for chunk in range(4):
            copies.put(r.lines_half.at[index, chunk], target.at[chunk, first : first + LINE_ROWS])


def pack_square(cfg, index, piece, target, first):
    true = cfg.true
    row = first + index // 2 * true
    col = index % 2 * true
    target[row : row + true, col : col + true] = piece[0:true, 0:true]


ANY = pl.BlockSpec(memory_space=pl.ANY)
NEAR = pl.BlockSpec(memory_space=pltpu.VMEM)
SCALAR = pl.BlockSpec(memory_space=pltpu.SMEM)


def shape(dims, dtype):
    return jax.ShapeDtypeStruct(dims, dtype)


def call(name, kernel, in_specs, outs, out_specs, scratch, flops, moved):
    return pl.pallas_call(
        kernel,
        name=name,
        out_shape=outs,
        in_specs=in_specs,
        out_specs=out_specs,
        scratch_shapes=scratch,
        compiler_params=pltpu.CompilerParams(vmem_limit_bytes=VMEM_BYTES),
        cost_estimate=pl.CostEstimate(flops=flops, bytes_accessed=moved, transcendentals=0),
    )


def named_call(name, body, ins, outs, scratch, flops, aliases=()):
    names = [entry[0] for entry in ins + outs + scratch]
    positions = {entry[0]: index for index, entry in enumerate(ins)}
    places = {entry[0]: index for index, entry in enumerate(outs)}

    def kernel(*refs):
        body(types.SimpleNamespace(**dict(zip(names, refs))))

    results = pl.pallas_call(
        kernel,
        name=name,
        out_shape=[entry[1] for entry in outs],
        in_specs=[entry[2] for entry in ins],
        out_specs=[entry[2] for entry in outs],
        scratch_shapes=[entry[1] for entry in scratch],
        input_output_aliases={positions[source]: places[target] for source, target in aliases},
        compiler_params=pltpu.CompilerParams(vmem_limit_bytes=VMEM_BYTES),
        cost_estimate=pl.CostEstimate(flops=flops, bytes_accessed=10**7, transcendentals=0),
    )(*[entry[1] for entry in ins])
    return {entry[0]: result for entry, result in zip(outs, results)}


def sizes(cfg):
    total = cfg.images * cfg.rows
    return total, total + WINDOW - cfg.rows, cfg.width


def semaphores(count):
    return pltpu.SemaphoreType.DMA((count,))


def block_shapes(cfg):
    total, longer, width = sizes(cfg)
    wide = shape((total, width), SINGLE)
    narrow = shape((total, width), HALF)
    inner = shape((total, cfg.hidden), HALF)
    return {
        "x": wide,
        "middle": wide,
        "y": wide,
        "grad": wide,
        "result": wide,
        "grad_x": wide,
        "mixed": shape((longer, 3 * width), HALF),
        "probs": shape((cfg.images * HEADS, cfg.rows, WINDOW), HALF),
        HEADS_AXIS: narrow,
        "normed": narrow,
        "branch": narrow,
        "active": inner,
        "slope": inner,
        "inner": inner,
        "grad_heads": shape((longer, width), HALF),
        "grad_mixed": shape((total, 3 * width), HALF),
        "qkv": shape((width, 3 * width), HALF),
        "out": shape((width, width), HALF),
        "up": shape((width, cfg.hidden), HALF),
        "down": shape((cfg.hidden, width), HALF),
        "pieces_mlp": shape((2, width, cfg.hidden), HALF),
        "pieces_attn": shape((4 * width, width) if cfg.true == width else (2 * cfg.true, 2 * cfg.true), HALF),
        "packed": shape((4, cfg.true, 2 * cfg.true), HALF),
        "ready": shape((2, 4, LINE_ROWS, width), SINGLE),
        "lines_half": shape((2, 4, LINE_ROWS, width), HALF),
        "landing": shape(tokens_shape(cfg), HALF),
    }


def block_call(name, cfg, body, ins, outs, scratch, aliases=()):
    shapes = block_shapes(cfg)
    names = list(dict.fromkeys(scratch))
    scratch = [(entry, pltpu.VMEM(shapes[entry].shape, shapes[entry].dtype)) for entry in names]
    scratch.append(("semaphores", semaphores(56)))
    outs = [entry if len(entry) == 3 else (entry[0], shapes[entry[0][:-4]], ANY) for entry in outs]
    flops = (20 if name == "forward" else 40) * cfg.images * cfg.rows * cfg.width**2
    return named_call(name, body, ins, outs, scratch, flops, aliases)


def shard_ins(shards):
    return [(name, shard, ANY) for name, shard in zip(("own", "core", "far", "both"), shards)]


def block_forward(cfg, x, params, shards=None, place=None, middle=None):
    layer, gain_attn, qkv, out, gain_mlp = params
    attn, mlp = middle is None, shards is not None
    ins, outs, scratch = [], [], []
    if attn:
        ins += [("gain_attn", gain_attn, NEAR), ("qkv_in", qkv, ANY), ("out_in", out, ANY)]
        if place is None:
            ins.append(("x_in", x, ANY))
        else:
            ins += [("tokens", x, ANY), ("place", place, SCALAR)]
            outs.append(("x_out",))
            scratch.append("landing")
        outs += [(MIDDLE,), ("mixed_out",), ("probs_out",), ("heads_out",)]
        scratch += ["x", "qkv", "out", "mixed", "probs", HEADS_AXIS, "normed"]
    else:
        ins.append(("middle_in", middle, ANY))
    if mlp:
        ins += [("gain_mlp", gain_mlp, NEAR)] + shard_ins(shards)
        outs += [(Y_OUT,), ("active_out",), ("slope_out",)]
        scratch += ["up", "down", "active", "slope", "y"]
    scratch.append("middle")
    kept = block_call("forward", cfg, functools.partial(forward_body, cfg, layer, attn, mlp), ins, outs, scratch)
    if attn and place is None:
        kept["x_out"] = x
    if not attn:
        kept[MIDDLE] = middle
    return kept


def block_backward(cfg, place, grad, kept, params, shards, attn=True, mlp=True, last=False, lines=None):
    layer, gain_attn, qkv, out, gain_mlp = params
    packed = cfg.true != cfg.width
    ins, outs, scratch = [("place", place, SCALAR)], [], ["result", "branch", "normed"]
    rows = 0
    if mlp:
        ins += [("grad_in", grad, ANY), ("gain_mlp", gain_mlp, NEAR)] + shard_ins(shards)
        ins += [(name + "_in", kept[name + "_out"], ANY) for name in ("middle", "active", "slope")]
        outs.append((GAIN_MLP, shape((1, cfg.width), SINGLE), NEAR))
        scratch += ["grad", "middle", "active", "slope", "up", "down", "inner", "pieces_mlp"]
        scratch += ["packed"] if packed else []
        rows += cfg.true // 2 if packed else cfg.width
        if not attn:
            outs.append((RESULT,))
    first_row = rows
    if attn:
        ins += [("gain_attn", gain_attn, NEAR), ("qkv_in", qkv, ANY), ("out_in", out, ANY)]
        ins += [(name + "_in", kept[name + "_out"], ANY) for name in ("x", "mixed", "probs", HEADS_AXIS)]
        if not mlp:
            ins.append(("result_in", grad, ANY))
        outs.append((GAIN_ATTN, shape((1, cfg.width), SINGLE), NEAR))
        if last:
            outs.append((GRAD_X, shape(tokens_shape(cfg), HALF), NEAR))
        else:
            outs.append((GRAD_X,))
        rows += cfg.true // 4 if packed else cfg.width // 2
        scratch += ["x", "mixed", "probs", HEADS_AXIS, "qkv", "out", "grad_heads", "grad_mixed", "grad_x", "pieces_attn"]
        if lines is not None:
            ins.append(("lines", lines, NEAR))
            scratch += ["ready", "lines_half"]
            rows += LINE_ROWS
    chunk = shape((4, rows, 2 * cfg.true if packed else cfg.width), HALF)
    outs += [(KEEP, chunk, ANY), (SEND, chunk, ANY)]
    body = functools.partial(backward_body, cfg, layer, attn, mlp, last, first_row)
    return block_call("backward", cfg, body, ins, outs, scratch)


def class_rows(ref, cfg):
    rows = [ref[image * cfg.rows : image * cfg.rows + 1, :] for image in range(cfg.images)]
    rows.append(jnp.zeros((CLS_ROWS - cfg.images, ref.shape[1]), ref.dtype))
    return jnp.concatenate(rows, axis=0)


def pack_rows(rows, images):
    rows.append(jnp.zeros((CLS_ROWS - images, rows[0].shape[1]), rows[0].dtype))
    return jnp.concatenate(rows, axis=0)


def unite_part(
    own, other, own_ref, other_ref, own_cot, weights, grads, unit, normed, keyval, grad_keyval, grad_patch
):
    gain_in, lift, gain_attn, qkv, out, gain_back, revert = weights
    g_in, g_attn, g_back, pack = grads
    images, rows, width = other.images, other.rows, other.width
    own_small = own.true < other.true
    total = images * rows
    size = other.true // HEADS
    scale = size ** (-0.5)
    lane = iota((CLS_ROWS, width), 1)
    head_low = iota((CLS_ROWS, width), 0) * size
    head_mask = ((lane >= head_low) & (lane < head_low + size) & (lane < other.true)).astype(SINGLE)
    key_ok = iota((CLS_ROWS, WINDOW), 1) < other.length

    unit_in, scale_in = norm(class_rows(own_ref, own), own.true)
    lifted_in, slope_in = gelu_both(unit_in * gain_in[...])
    lifted_in = lifted_in.astype(HALF)
    lifted = dot(lifted_in, lift[...])
    unit_cls, scale_cls = norm(lifted, other.true)
    normed_cls = (unit_cls * gain_attn[...]).astype(HALF)

    for image in range(images):
        at = slice(image * rows, (image + 1) * rows)
        here = jnp.where(
            iota((rows, 1), 0) == 0, lifted[image : image + 1], other_ref[at, :]
        )
        unit_here, scale_here = norm(here, other.true)
        unit[at, :] = unit_here
        grad_patch[at, :] = jnp.broadcast_to(scale_here, (rows, width))
        normed[at, :] = (unit_here * gain_attn[...]).astype(HALF)

    for part in range(2):
        cols = slice(part * width, (part + 1) * width)
        keyval[0:total, cols] = dot(
            normed[...], qkv[:, (part + 1) * width : (part + 2) * width]
        ).astype(HALF)
    keyval[total:, :] = jnp.zeros((keyval.shape[0] - total, 2 * width), HALF)
    query = dot(normed_cls, qkv[:, 0:width]).astype(HALF).astype(SINGLE)
    queries, probs_all, probs_half, merged = [], [], [], []
    for image in range(images):
        window = slice(image * rows, image * rows + WINDOW)
        spread = (head_mask * query[image : image + 1]).astype(HALF)
        scores = dot_nt(spread, keyval[window, 0:width]) * scale
        scores = jnp.where(key_ok, scores, NEG)
        raised = jnp.exp(scores - jnp.max(scores, axis=1, keepdims=True))
        prob = raised / jnp.sum(raised, axis=1, keepdims=True)
        half = prob.astype(HALF)
        mixed = dot(half, keyval[window, width : 2 * width])
        merged.append(jnp.sum(mixed * head_mask, axis=0, keepdims=True))
        queries.append(spread)
        probs_all.append(prob)
        probs_half.append(half)
    merged = pack_rows(merged, images).astype(HALF)
    calibrated = lifted + dot(merged, out[...])
    unit_back, scale_back = norm(calibrated, other.true)
    back_in, slope_back = gelu_both(unit_back * gain_back[...])
    back_in = back_in.astype(HALF)
    result = dot(back_in, revert[...])

    grad_final = class_rows(own_cot, own).astype(HALF)
    g_revert = dot_tn(grad_final, back_in) if own_small else dot_tn(back_in, grad_final)
    grad_back = dot_nt(grad_final, revert[...]) * slope_back
    g_back[...] = jnp.sum(grad_back * unit_back, axis=0, keepdims=True)
    grad_cal = norm_back(grad_back * gain_back[...], unit_back, scale_back, other.true)
    grad_cross = grad_cal.astype(HALF)
    g_out = dot_tn(merged, grad_cross).astype(HALF)
    grad_merged = dot_nt(grad_cross, out[...]).astype(HALF).astype(SINGLE)
    grad_query = []
    for image in range(images):
        window = slice(image * rows, image * rows + WINDOW)
        at = slice(image * rows, (image + 1) * rows)
        spread = (head_mask * grad_merged[image : image + 1]).astype(HALF)
        grad_prob = dot_nt(spread, keyval[window, width : 2 * width])
        prob = probs_all[image]
        along = jnp.sum(prob * grad_prob, axis=1, keepdims=True)
        grad_score = (prob * (grad_prob - along)).astype(HALF)
        back = dot(grad_score, keyval[window, 0:width]) * head_mask
        grad_query.append(jnp.sum(back, axis=0, keepdims=True) * scale)
        grad_key = dot_tn(grad_score, queries[image]) * scale
        grad_value = dot_tn(probs_half[image], spread)
        grad_keyval[at, 0:width] = grad_key[:rows].astype(HALF)
        grad_keyval[at, width : 2 * width] = grad_value[:rows].astype(HALF)
    grad_query = pack_rows(grad_query, images).astype(HALF)
    g_qkv = [dot_tn(normed_cls, grad_query).astype(HALF)]
    for part in range(2):
        cols = slice(part * width, (part + 1) * width)
        g_qkv.append(dot_tn(normed[...], grad_keyval[:, cols]).astype(HALF))
    from_query = dot_nt(grad_query, qkv[:, 0:width])
    gain_total = jnp.zeros((1, width), SINGLE)
    grad_lifted = []
    for image in range(images):
        at = slice(image * rows, (image + 1) * rows)
        grad = dot_nt(grad_keyval[at, :], qkv[:, width : 3 * width])
        grad = grad + jnp.where(iota((rows, 1), 0) == 0, from_query[image : image + 1], 0.0)
        unit_here = unit[at, :]
        gain_total = gain_total + jnp.sum(grad * unit_here, axis=0, keepdims=True)
        scale_here = grad_patch[at, :]
        back = norm_back(grad * gain_attn[...], unit_here, scale_here, other.true)
        grad_patch[at, :] = back
        grad_lifted.append(back[0:1])
    g_attn[...] = gain_total
    grad_lifted = (grad_cal + pack_rows(grad_lifted, images)).astype(HALF)
    g_lift = dot_tn(lifted_in, grad_lifted) if own_small else dot_tn(grad_lifted, lifted_in)
    grad_in = dot_nt(grad_lifted, lift[...]) * slope_in
    g_in[...] = jnp.sum(grad_in * unit_in, axis=0, keepdims=True)
    grad_cls = norm_back(grad_in * gain_in[...], unit_in, scale_in, own.true)
    narrow = min(own.true, other.true)
    wide = max(own.true, other.true)
    target, row = pack
    for piece in (g_lift, g_revert):
        target[row : row + narrow, :] = piece[0:narrow, :].astype(HALF)
        row += narrow
    if own_small:
        for piece in g_qkv + [g_out]:
            target[row : row + wide, :] = piece
            row += wide
    else:
        for index, piece in enumerate(g_qkv + [g_out]):
            pack_square(other, index, piece, target, row)
    return result, grad_cls


def finish_rows(cfg, mid_ref, cot_ref, result, grad_cls, result_ref, grad_ref):
    for image in range(cfg.images):
        at = slice(image * cfg.rows, (image + 1) * cfg.rows)
        first = iota((cfg.rows, 1), 0) == 0
        rows = jnp.where(first, result[image : image + 1], mid_ref[at, :])
        put_tokens(cfg, result_ref, image, rows)
        grad_ref[at, :] = jnp.where(
            first, grad_cls[image : image + 1], grad_ref[at, :] + cot_ref[at, :]
        )


def unite_rows(small, large):
    first = 2 * small.true + 4 * large.true
    used = first + 4 * small.true
    return first, used, round_up(used, 512)


def unite_kernel(small, large, *refs):
    place, small_tokens, large_tokens, small_mid, large_mid = refs[0:5]
    first, second = refs[5:12], refs[12:19]
    small_res, large_res, grad_small, grad_large, keep, send = refs[19:25]
    first_gains, second_gains = refs[25:28], refs[28:31]
    first_work, second_work = refs[31:35], refs[35:39]
    small_land, large_land, small_cot, large_cot, packed, sems = refs[39:]
    begin, used, rows = unite_rows(small, large)
    copies = Copies(sems)
    load_tokens(small, place, small_tokens, small_land, small_cot, copies)
    load_tokens(large, place, large_tokens, large_land, large_cot, copies)
    packed[used:rows, :] = jnp.zeros((rows - used, packed.shape[1]), HALF)
    small_head, grad_small_cls = unite_part(
        small, large, small_mid, large_mid, small_cot, first, (*first_gains, (packed, 0)), *first_work, grad_large
    )
    large_head, grad_large_cls = unite_part(
        large, small, large_mid, small_mid, large_cot, second, (*second_gains, (packed, begin)), *second_work,
        grad_small,
    )
    put_rows(place, packed, 0, keep, send, 0, copies)
    finish_rows(small, small_mid, small_cot, small_head, grad_small_cls, small_res, grad_small)
    finish_rows(large, large_mid, large_cot, large_head, grad_large_cls, large_res, grad_large)
    copies.finish()


def unite_both(small, large, place, small_cot, large_cot, small_mid, large_mid, first, second):
    def gains(own, other):
        return [shape((1, own.width), SINGLE), shape((1, other.width), SINGLE), shape((1, other.width), SINGLE)]

    def work(other):
        total, longer, width = sizes(other)
        return [
            pltpu.VMEM((total, width), SINGLE),
            pltpu.VMEM((total, width), HALF),
            pltpu.VMEM((longer, 2 * width), HALF),
            pltpu.VMEM((total, 2 * width), HALF),
        ]

    def rows(cfg):
        return shape((cfg.images * cfg.rows, cfg.width), SINGLE)

    def tokens(cfg):
        return shape(tokens_shape(cfg), HALF)

    outs = [tokens(small), tokens(large), rows(small), rows(large)]
    packed = unite_rows(small, large)[2]
    outs += [shape((4, packed // 8, large.width), HALF)] * 2
    outs += gains(small, large) + gains(large, small)
    scratch = work(large) + work(small)
    for cfg in (small, large):
        scratch.append(pltpu.VMEM(tokens_shape(cfg), HALF))
    for cfg in (small, large):
        scratch.append(pltpu.VMEM((cfg.images * cfg.rows, cfg.width), SINGLE))
    scratch += [pltpu.VMEM((packed, large.width), HALF), semaphores(10)]
    return call(
        "unite", functools.partial(unite_kernel, small, large), [SCALAR, ANY, ANY] + [NEAR] * 16, outs,
        [NEAR] * 4 + [ANY] * 2 + [NEAR] * 6, scratch, 30 * large.images * large.rows * large.width**2, 10**7,
    )(place, small_cot, large_cot, small_mid, large_mid, *first, *second)


def pad_dims(array, dims):
    return jnp.pad(array, [(0, dim - old) for old, dim in zip(array.shape, dims)])


def prepare_kernel(small, large, *refs):
    ins, outs, up, down, sems = refs[0:20], refs[20:-3], refs[-3], refs[-2], refs[-1]
    stacked = outs[17:]
    copies = Copies(sems)
    gets = []
    for layer in range(len(stacked)):
        gets.append(copies.begin(ins[18].at[layer], up.at[layer]))
        gets.append(copies.begin(ins[19].at[layer], down.at[layer]))
    for layer, target in enumerate(stacked):
        gets[2 * layer].wait()
        copies.put(up.at[layer], target.at[0])
        gets[2 * layer + 1].wait()
        copies.put(down.at[layer], target.at[1])
    shard = outs[16]
    shard[...] = jnp.zeros(shard.shape, HALF)
    for index in range(2):
        matrix = ins[16 + index]
        shard[index, 0 : matrix.shape[0], 0 : matrix.shape[1]] = matrix[...]
    for source, target in zip(ins[0:16], outs[0:16]):
        tall, wide = source.shape
        target[...] = jnp.zeros(target.shape, target.dtype)
        if wide == 3 * small.true and tall == small.true:
            for part in range(3):
                cols = slice(part * small.width, part * small.width + tall)
                target[0:tall, cols] = source[:, part * tall : (part + 1) * tall]
        elif tall == small.true and target.shape[0] == large.width:
            target[0:wide, 0:tall] = source[...].astype(SINGLE).T.astype(target.dtype)
        else:
            target[0:tall, 0:wide] = source[...]
    copies.finish()


def prepare(small, large, small_params, first, second, large_up, large_down):
    gain_attn, qkv, out, gain_mlp, up, down = small_params
    depth = large_up.shape[0]
    ns, nl = small.width, large.width
    squares = [gain_attn[None], qkv, out, gain_mlp[None]]
    sizes_out = [(1, ns), (ns, 3 * ns), (ns, ns), (1, ns)]

    def unite_pads(weights, own, other):
        gain_in, lift, gain, qkv, out, gain_back, revert = weights
        lift, revert = [matrix.T if matrix.shape[0] > matrix.shape[1] else matrix for matrix in (lift, revert)]
        arrays = [gain_in[None], lift, gain[None], out, gain_back[None], revert]
        shapes = [(1, own), (own, other), (1, other), (other, other), (1, other), (other, own)]
        return arrays, shapes, qkv, (other, 3 * other)

    first_arrays, first_shapes, first_qkv, _ = unite_pads(first, ns, nl)
    second_arrays, second_shapes, second_qkv, second_dims = unite_pads(second, nl, ns)
    need = [0, 1, 5]
    arrays = squares + [first_arrays[index] for index in need] + second_arrays + [second_qkv]
    dims = sizes_out + [first_shapes[index] for index in need] + second_shapes + [second_dims]
    extra = 16 - len(arrays)
    arrays += [gain_attn[None]] * extra
    dims += [(1, ns)] * extra
    outs = [shape(size, array.dtype) for size, array in zip(dims, arrays)]
    outs += [shape((2, ns, small.hidden // 4), HALF)]
    outs += [shape((2, nl, nl), HALF)] * depth
    results = call(
        "prepare", functools.partial(prepare_kernel, small, large), [NEAR] * 18 + [ANY] * 2, outs,
        [NEAR] * 17 + [ANY] * depth,
        [pltpu.VMEM(large_up.shape, HALF), pltpu.VMEM(large_down.shape, HALF), semaphores(4 * depth)], 10**6, 10**7,
    )(*arrays, up, down, large_up, large_down)
    small_ready = results[0:4]
    f_in, f_lift, f_revert = results[4:7]
    s_in, s_lift, s_attn, s_out, s_back, s_revert, s_qkv = results[7:14]
    first_ready = (f_in, f_lift, first_arrays[2], first_qkv, first_arrays[3], first_arrays[4], f_revert)
    second_ready = (s_in, s_lift, s_attn, s_qkv, s_out, s_back, s_revert)
    return small_ready, first_ready, second_ready, results[16], results[17:]


def plus(*terms):
    total = terms[0].astype(SINGLE)
    for term in terms[1:]:
        total = total + term.astype(SINGLE)
    return total.astype(HALF)


class Links:
    def __init__(self):
        heads, dp = lax.axis_size(HEADS_AXIS), lax.axis_size(ROW_AXIS)
        place, row = lax.axis_index(HEADS_AXIS), lax.axis_index(ROW_AXIS)
        self.heads, self.dp = heads, dp
        self.core, self.far, self.side = place % 2, place // 2, row % 2

    def scalars(self):
        place = lax.axis_index(HEADS_AXIS)
        return jnp.stack([place, self.side, self.far, self.core]).astype(jnp.int32)

    def swap(self, array, axis, bit):
        size = self.heads if axis == HEADS_AXIS else self.dp
        return lax.ppermute(array, axis, [(index, index ^ bit) for index in range(size)])

    def by_core(self, array):
        return self.swap(array, HEADS_AXIS, 1)

    def by_far(self, array):
        return self.swap(array, HEADS_AXIS, 2)

    def by_side(self, array):
        return self.swap(array, ROW_AXIS, 1)

    def long_steps(self):
        bits = [2 << step for step in range((self.dp // 2).bit_length() - 1)]
        if len(bits) == 2:
            bits = [2, 6]
        return [functools.partial(self.swap, axis=ROW_AXIS, bit=bit) for bit in bits]


def whole(mine, other, index):
    return jnp.where(index == 0, jnp.stack([mine, other]), jnp.stack([other, mine]))


def reduce_steps(links, keep, send, shared, side_first=False):
    owned = keep.shape[1] - shared
    lanes = keep.shape[2]
    outer, inner = (links.by_far, links.far), (links.by_side, links.side)
    if side_first:
        outer, inner = inner, outer
    (send,) = yield [send]
    got = links.by_core(send)
    away, own = yield [plus(keep[2:4], got[2:4]), plus(keep[0:2], got[0:2])]
    got = outer[0](away)
    away, own = yield [plus(own[1], got[1]), plus(own[0], got[0])]
    (own,) = yield [plus(own, inner[0](away))]
    for step in links.long_steps():
        (own,) = yield [plus(own, step(own))]
    got = inner[0](own)
    hidden = whole(own[:owned], got[:owned], inner[1]) if owned else None
    if not shared:
        return hidden, None
    (mine,) = yield [whole(own[owned:], got[owned:], inner[1]).reshape(-1, lanes)]
    (mine,) = yield [whole(mine, outer[0](mine), outer[1]).reshape(-1, lanes)]
    return hidden, whole(mine, links.by_core(mine), links.core).reshape(-1, lanes)


class Rounds:
    def __init__(self):
        self.active = {}
        self.waiting = {}
        self.done = {}

    def add(self, name, steps):
        self.active[name] = steps
        self.waiting[name] = next(steps)

    def tie(self, names, *arrays):
        names = [name for name in (self.active if names is None else names) if name in self.active]
        held = {name: self.waiting[name] for name in names}
        if held:
            arrays, held = lax.optimization_barrier((arrays, held))
        for name in names:
            try:
                self.waiting[name] = self.active[name].send(held[name])
            except StopIteration as stop:
                self.done[name] = stop.value
                del self.active[name], self.waiting[name]
        return arrays if len(arrays) != 1 else arrays[0]


def per_device(
    small_tokens,
    large_tokens,
    small_cotangent,
    large_cotangent,
    small_gain_attn,
    small_qkv,
    small_out,
    small_gain_mlp,
    small_up,
    small_down,
    large_gain_attn,
    large_qkv,
    large_out,
    large_gain_mlp,
    large_up,
    large_down,
    *unite_weights,
):
    devices = lax.axis_size(HEADS_AXIS)
    depth = large_qkv.shape[0]
    images = small_tokens.shape[0] // devices
    links = Links()
    place = links.scalars()

    def branch(tokens, hidden):
        _, length, true = tokens.shape
        return Branch(images, round_up(length, 16), length, round_up(true, LANES), true, hidden * devices)

    small = branch(small_tokens, round_up(small_up.shape[1], LANES))
    large = branch(large_tokens, large_up.shape[2])
    small_ready, first, second, small_shard, large_shards = prepare(
        small,
        large,
        (small_gain_attn, small_qkv, small_out, small_gain_mlp, small_up, small_down),
        unite_weights[0:7],
        unite_weights[7:14],
        large_up,
        large_down,
    )

    def after(value, *others):
        return lax.optimization_barrier((value, *others))[0]

    def spread(shard, far):
        return (shard, links.by_core(shard), far, links.by_core(far))

    far_small = links.by_far(small_shard)
    far = [links.by_far(large_shards[0])]
    large_gains = [(large_gain_attn[layer][None], large_gain_mlp[layer][None]) for layer in range(depth)]

    small_block = (None, *small_ready[0:4])
    large_blocks = [
        (layer, large_gains[layer][0], large_qkv, large_out, large_gains[layer][1]) for layer in range(depth)
    ]
    small_tokens, small_cotangent = small_tokens.swapaxes(1, 2), small_cotangent.swapaxes(1, 2)
    small_kept = block_forward(small, small_tokens, small_block, None, place)
    tokens, small_kept[MIDDLE] = lax.optimization_barrier((large_tokens, small_kept[MIDDLE]))
    large_kept, large_weights = [], []
    kept = block_forward(large, tokens, large_blocks[0], None, place)
    small_middle, middle, far[0], far_small = lax.optimization_barrier(
        (small_kept[MIDDLE], kept[MIDDLE], far[0], far_small)
    )
    small_weights = spread(small_shard, far_small)
    large_weights.append(spread(large_shards[0], far[0]))
    far.append(links.by_far(after(large_shards[1], far[0])))
    small_kept |= block_forward(small, None, small_block, small_weights, None, small_middle)
    middle = after(middle, small_kept[Y_OUT])
    kept |= block_forward(large, None, large_blocks[0], large_weights[0], None, middle)
    large_kept.append(kept)
    state = kept[Y_OUT]
    for layer in range(1, depth):
        state, far[layer] = lax.optimization_barrier((state, far[layer]))
        large_weights.append(spread(large_shards[layer], far[layer]))
        if layer + 1 < depth:
            far.append(links.by_far(after(large_shards[layer + 1], far[layer])))
        large_kept.append(block_forward(large, state, large_blocks[layer], large_weights[layer]))
        state = large_kept[layer][Y_OUT]
    small_mid = small_kept[Y_OUT]

    small_res, large_res, grad_small, grad, keep, send, *unite_gains = unite_both(
        small, large, place, small_cotangent, large_cotangent, small_mid, state, first, second
    )

    def gather(array):
        return lax.all_gather(array, HEADS_AXIS, axis=0, tiled=True)

    small_result, large_result = gather(small_res).swapaxes(1, 2), gather(large_res)
    rounds = Rounds()
    rounds.add("unite", reduce_steps(links, keep, send, keep.shape[1]))
    gains = [None] * depth
    lanes = large.width

    def large_back(layer):
        names = [name for name in rounds.active if layer != 1 or name != "large2"]
        back = block_backward(large, place, rounds.tie(names, grad), large_kept[layer], large_blocks[layer], large_weights[layer])
        gains[layer] = (back[GAIN_ATTN], back[GAIN_MLP])
        rounds.add("large%d" % layer, reduce_steps(links, back[KEEP], back[SEND], lanes // 2))
        return back[GRAD_X]

    for layer in range(depth - 1, 0, -1):
        if layer == 1:
            grad, grad_small = lax.optimization_barrier((grad, grad_small))
            grad_small = rounds.tie(None, grad_small)
            back = block_backward(small, place, grad_small, small_kept, small_block, small_weights, last=True)
            rounds.add("small", reduce_steps(links, back[KEEP], back[SEND], small.true // 4))
            small_grad = gather(back[GRAD_X]).swapaxes(1, 2).astype(SINGLE)
            small_gains = [back[GAIN_ATTN], back[GAIN_MLP]]
            grad, small_gains = lax.optimization_barrier((grad, small_gains))
        grad = large_back(layer)
    grad = rounds.tie(None, grad)
    back = block_backward(large, place, grad, large_kept[0], large_blocks[0], large_weights[0], attn=False)
    rounds.add("hidden0", reduce_steps(links, back[KEEP], back[SEND], 0))
    gains[0] = (jnp.zeros((1, lanes), SINGLE), back[GAIN_MLP])
    lines = [gain for pair in gains for gain in pair] + small_gains + unite_gains
    lines = jnp.concatenate([pad_dims(line, (1, lanes)) for line in lines])
    lines = pad_dims(lines, (round_up(lines.shape[0], 8), lanes))
    grad = rounds.tie(None, back[RESULT])
    back = block_backward(
        large, place, grad, large_kept[0], large_blocks[0], None, mlp=False, last=True, lines=lines
    )
    rounds.add("large0", reduce_steps(links, back[KEEP], back[SEND], lanes // 2 + LINE_ROWS, True))
    large_grad = gather(back[GRAD_X]).astype(SINGLE)
    while rounds.active:
        rounds.tie(None)

    true = small.true

    def square(rows):
        (q, k), (v, o) = [jnp.split(half, 2, axis=1) for half in jnp.split(rows, 2, axis=0)]
        return jnp.concatenate([q, k, v], axis=1), o

    def full(rows):
        q, k, v, o = jnp.split(rows, 4, axis=0)
        return jnp.concatenate([q, k, v], axis=1), o

    s_hidden, s_rest = rounds.done["small"]
    s_hidden = s_hidden.reshape(true, 2 * true).astype(SINGLE)
    s_qkv, s_out = square(s_rest.astype(SINGLE))
    count = lines.shape[0] // 8
    last = rounds.done["large0"][1].reshape(8, -1, lanes)
    line = last[:, lanes // 2 : lanes // 2 + count].reshape(8 * count, lanes).astype(SINGLE)
    first_rest = last[:, : lanes // 2].reshape(4 * lanes, lanes)
    at = 2 * depth
    l_hidden = [rounds.done["large%d" % layer if layer else "hidden0"][0] for layer in range(depth)]
    l_rest = [full(rounds.done["large%d" % layer][1] if layer else first_rest) for layer in range(depth)]
    u_rest = rounds.done["unite"][1].astype(SINGLE)
    begin, used, _ = unite_rows(small, large)
    f_qkv, f_out = full(u_rest[2 * true : begin])
    u_second = u_rest[begin:used]
    e_qkv, e_out = square(u_second[2 * true :])
    return (
        small_result,
        large_result,
        small_grad,
        large_grad,
        line[at, :true],
        s_qkv,
        s_out,
        line[at + 1, :true],
        s_hidden[:, :true],
        s_hidden[:, true:].T,
        line[0:at:2],
        jnp.stack([pair[0] for pair in l_rest]).astype(SINGLE),
        jnp.stack([pair[1] for pair in l_rest]).astype(SINGLE),
        line[1:at:2],
        jnp.stack([pair[0] for pair in l_hidden]).astype(SINGLE),
        jnp.stack([pair[1] for pair in l_hidden]).swapaxes(1, 2).astype(SINGLE),
        line[at + 2, :true],
        u_rest[:true],
        line[at + 3],
        f_qkv,
        f_out,
        line[at + 4],
        u_rest[true : 2 * true].T,
        line[at + 5],
        u_second[:true].T,
        line[at + 6, :true],
        e_qkv,
        e_out,
        line[at + 7, :true],
        u_second[true : 2 * true],
    )


def solution(mesh):
    rows = P(ROW_AXIS, None, None)
    copied = P()
    split = [copied] * 4 + [P(None, HEADS_AXIS), P(HEADS_AXIS, None)]
    stack = [copied] * 4 + [P(None, None, HEADS_AXIS), P(None, HEADS_AXIS, None)]
    specs = tuple([rows] * 4 + split + stack + [copied] * 14)
    return jax.shard_map(per_device, mesh=mesh, in_specs=specs, out_specs=specs, check_vma=False)
```

```python
import collections
import functools
import types

import jax
import jax.numpy as jnp
from jax import lax
from jax.experimental import pallas as pl
from jax.experimental.pallas import tpu as pltpu
from jax.sharding import PartitionSpec as P

HEADS_AXIS, ROW_AXIS = "heads", "dp"
MIDDLE, RESULT, Y_OUT, GRAD_X = "middle_out", "result_out", "y_out", "grad_x_out"
KEEP, SEND, GAIN_ATTN, GAIN_MLP = "keep_out", "send_out", "gain_attn_out", "gain_mlp_out"
EPS = 1e-06
SINGLE = jnp.float32
HALF = jnp.bfloat16
HEADS = 6
LANES = 128
WINDOW = 256
CLS_ROWS = 16
NEG = -1e30
ROOT_HALF = 0.7071067811865476
INV_ROOT_2PI = 0.3989422804014327
VMEM_BYTES = 60 * 1024 * 1024
FORWARD_UNROLL = 4
LINE_ROWS = 16
BACKWARD_UNROLL = 4

Branch = collections.namedtuple("Branch", ("images", "rows", "length", "width", "true", "hidden"))


def round_up(value, step):
    return -(-value // step) * step


def dot(left, right):
    return jnp.dot(left, right, preferred_element_type=SINGLE)


def dot_nt(left, right):
    return lax.dot_general(left, right, (((1,), (1,)), ((), ())), preferred_element_type=SINGLE)


def dot_tn(left, right):
    return lax.dot_general(left, right, (((0,), (0,)), ((), ())), preferred_element_type=SINGLE)


def iota(shape, dim):
    return lax.broadcasted_iota(jnp.int32, shape, dim)


def norm(values, true):
    width = values.shape[-1]
    mean = jnp.sum(values, axis=-1, keepdims=True) * (1.0 / true)
    center = values - mean
    if true != width:
        center = jnp.where(iota((1, width), 1) < true, center, 0.0)
    spread = jnp.sum(center * center, axis=-1, keepdims=True) * (1.0 / true)
    scale = lax.rsqrt(spread + EPS)
    return center * scale, scale


def norm_back(grad, unit, scale, true):
    mean = jnp.sum(grad, axis=-1, keepdims=True) * (1.0 / true)
    along = jnp.sum(grad * unit, axis=-1, keepdims=True) * (1.0 / true)
    return scale * (grad - mean - unit * along)


def gelu_both(values):
    phi = 0.5 + 0.5 * lax.erf(values * ROOT_HALF)
    density = jnp.exp(values * values * -0.5) * INV_ROOT_2PI
    return values * phi, phi + values * density


def heads_of(cfg, block):
    size = cfg.true // HEADS
    per = LANES // size
    first = block * per
    return size, [head for head in range(first, min(first + per, HEADS))]


def lane_mask(head, size):
    low = head * size % LANES
    lane = iota((1, LANES), 1)
    return (lane >= low) & (lane < low + size)


class Copies:
    def __init__(self, semaphores):
        self.semaphores, self.used, self.puts = semaphores, 0, []

    def begin(self, source, target):
        copy = pltpu.make_async_copy(source, target, self.semaphores.at[self.used])
        self.used += 1
        copy.start()
        return copy

    def put(self, source, target):
        self.puts.append(self.begin(source, target))

    def block(self, count):
        self.used += count
        return self.used - count

    def finish(self):
        for copy in self.puts:
            copy.wait()


def wait(copies):
    for copy in copies:
        copy.wait()


def flipped(cfg):
    return cfg.true != cfg.width


def tokens_shape(cfg):
    return (cfg.images, cfg.true, cfg.length) if flipped(cfg) else (cfg.images, cfg.length, cfg.true)


def put_tokens(cfg, target, image, rows):
    rows = rows.T if flipped(cfg) else rows
    target[image] = rows[0 : target.shape[1], 0 : target.shape[2]].astype(HALF)


def load_tokens(cfg, place, tokens, landing, target, copies):
    copy = copies.begin(tokens.at[pl.ds(place[0] * cfg.images, cfg.images)], landing)
    target[...] = jnp.zeros(target.shape, target.dtype)
    copy.wait()
    for image in range(cfg.images):
        first = image * cfg.rows
        rows = landing[image].astype(target.dtype)
        target[first : first + cfg.length, 0 : cfg.true] = rows.T if flipped(cfg) else rows


def shard_copies(cfg, copies, shards, target, index):
    size = cfg.hidden // 4
    gets = []
    for number, shard in enumerate(shards):
        part = slice(number * size, (number + 1) * size)
        gets.append(copies.begin(shard.at[index], target.at[:, part] if index == 0 else target.at[part, :]))
    return gets


def rows_of(cfg, image):
    return pl.ds(pl.multiple_of(image * cfg.rows, 16), cfg.rows)


def attention(cfg, mixed, heads, probs, image, key_ok, query_ok):
    rows, width = cfg.rows, cfg.width
    work = []
    for block in range(width // LANES):
        low = block * LANES
        base = pl.multiple_of(image * rows, 16)
        query = mixed[pl.ds(base, WINDOW), low : low + LANES]
        key = mixed[pl.ds(base, rows), width + low : width + low + LANES]
        size, here = heads_of(cfg, block)
        for head in here:
            masked = jnp.where(lane_mask(head, size), key, jnp.zeros_like(key))
            work.append(dot_nt(masked, query))
    order = 0
    for block in range(width // LANES):
        low = block * LANES
        base = pl.multiple_of(image * rows, 16)
        value_t = mixed[pl.ds(base, rows), 2 * width + low : 2 * width + low + LANES].T
        size, here = heads_of(cfg, block)
        pieces = []
        for head in here:
            scores = jnp.where(key_ok, work[order] * size ** (-0.5), NEG)
            order += 1
            top = jnp.max(scores, axis=0, keepdims=True)
            raised = jnp.exp(scores - top)
            total_row = jnp.sum(raised, axis=0, keepdims=True)
            prob = (raised * (query_ok / total_row)).astype(HALF)
            probs[image * HEADS + head] = prob
            first = head * size % LANES
            pieces.append(dot(value_t[first : first + size], prob))
        if len(here) * size < LANES:
            pieces.append(jnp.zeros((LANES - len(here) * size, WINDOW), SINGLE))
        heads[pl.ds(base, rows), low : low + LANES] = jnp.concatenate(pieces, axis=0).T[:rows].astype(HALF)


def forward_attn(cfg, r, copies, get_x, get_qkv, get_out):
    rows, width = cfg.rows, cfg.width
    total = cfg.images * rows
    wait(get_x)

    @pl.loop(0, cfg.images, unroll=True)
    def _(image):
        at = rows_of(cfg, image)
        unit, _ = norm(r.x[at, :], cfg.true)
        r.normed[at, :] = (unit * r.gain_attn[...]).astype(HALF)

    wait(get_qkv)
    for part in range(3):
        cols = slice(part * width, (part + 1) * width)
        r.mixed[0:total, cols] = dot(r.normed[...], r.qkv[:, cols]).astype(HALF)
    r.mixed[total:, :] = jnp.zeros((r.mixed.shape[0] - total, 3 * width), HALF)
    copies.put(r.mixed, r.mixed_out)

    key_ok = iota((rows, WINDOW), 0) < cfg.length
    query_ok = (iota((1, WINDOW), 1) < cfg.length).astype(SINGLE)

    @pl.loop(0, cfg.images // FORWARD_UNROLL)
    def _(step):
        for part in range(FORWARD_UNROLL):
            attention(cfg, r.mixed, r.heads, r.probs, step * FORWARD_UNROLL + part, key_ok, query_ok)

    copies.put(r.probs, r.probs_out)
    copies.put(r.heads, r.heads_out)
    wait(get_out)
    r.middle[...] = r.x[...] + dot(r.heads[...], r.out[...])
    copies.put(r.middle, r.middle_out)


def forward_mlp(cfg, r, copies, get_middle, get_up, get_down):
    first = copies.block(2 * cfg.images)
    wait(get_middle + get_up)

    def puts(image):
        at = rows_of(cfg, image)
        return [
            pltpu.make_async_copy(r.active.at[at], r.active_out.at[at], copies.semaphores.at[first + 2 * image]),
            pltpu.make_async_copy(r.slope.at[at], r.slope_out.at[at], copies.semaphores.at[first + 2 * image + 1]),
        ]

    @pl.loop(0, cfg.images, unroll=True)
    def _(image):
        at = rows_of(cfg, image)
        unit, _ = norm(r.middle[at, :], cfg.true)
        normed = (unit * r.gain_mlp[...]).astype(HALF)
        for low in range(0, cfg.hidden, WINDOW):
            cols = slice(low, low + WINDOW)
            act, grad = gelu_both(dot(normed, r.up[:, cols]))
            r.active[at, cols] = act.astype(HALF)
            r.slope[at, cols] = grad.astype(HALF)
        for copy in puts(image):
            copy.start()

    wait(get_down)
    half = cfg.images * cfg.rows // 2
    for part in range(2):
        at = slice(part * half, (part + 1) * half)
        r.y[at, :] = r.middle[at, :] + dot(r.active[at, :], r.down[...])
        copies.put(r.y.at[at], r.y_out.at[at])
    for image in range(cfg.images):
        wait(puts(image))


def pick_layer(layer, r):
    if layer is not None and hasattr(r, "qkv_in"):
        r.qkv_in, r.out_in = r.qkv_in.at[layer], r.out_in.at[layer]


def forward_body(cfg, layer, attn, mlp, r):
    pick_layer(layer, r)
    copies = Copies(r.semaphores)
    get_x = get_middle = get_up = get_down = []
    if attn:
        if hasattr(r, "tokens"):
            load_tokens(cfg, r.place, r.tokens, r.landing, r.x, copies)
            copies.put(r.x, r.x_out)
        else:
            get_x = [copies.begin(r.x_in, r.x)]
        get_qkv = [copies.begin(r.qkv_in, r.qkv)]
        get_out = [copies.begin(r.out_in, r.out)]
    else:
        get_middle = [copies.begin(r.middle_in, r.middle)]
    if mlp:
        shards = (r.own, r.core, r.far, r.both)
        get_up = shard_copies(cfg, copies, shards, r.up, 0)
        get_down = shard_copies(cfg, copies, shards, r.down, 1)
    if attn:
        forward_attn(cfg, r, copies, get_x, get_qkv, get_out)
    if mlp:
        forward_mlp(cfg, r, copies, get_middle, get_up, get_down)
    copies.finish()


def backward_mlp(cfg, r, copies, get):
    rows, width = cfg.rows, cfg.width
    size = cfg.hidden // 4
    wait(get["grad"])
    r.branch[...] = r.grad[...].astype(HALF)
    wait(get["down"] + get["slope"])

    @pl.loop(0, cfg.images, unroll=True)
    def _(image):
        at = rows_of(cfg, image)
        for low in range(0, cfg.hidden, WINDOW):
            cols = slice(low, low + WINDOW)
            grad_active = dot_nt(r.branch[at, :], r.down[cols, :])
            r.inner[at, cols] = (grad_active * r.slope[at, cols].astype(SINGLE)).astype(HALF)

    def put(index):
        for shard in range(4):
            target = (r.keep_out, r.send_out)[shard % 2]
            cols = slice(shard * size, (shard + 1) * size)
            if cfg.true == width:
                chunk = target.at[shard // 2 * 2 + lax.rem(r.place[1] + index, 2), 0:width]
                copies.put(r.pieces_mlp.at[index, :, cols], chunk)
            else:
                at = slice(index * cfg.true, (index + 1) * cfg.true)
                r.packed[shard, :, at] = r.pieces_mlp[index, 0 : cfg.true, cols][:, 0 : cfg.true]
                if index == 0:
                    half = cfg.true // 2
                    for side in range(2):
                        chunk = shard // 2 * 2 + lax.rem(r.place[1] + side, 2)
                        rows_here = slice(side * half, (side + 1) * half)
                        copies.put(r.packed.at[shard, rows_here], target.at[chunk, 0:half])

    wait(get["active"])
    r.pieces_mlp[1] = dot_tn(r.branch[...], r.active[...]).astype(HALF)
    put(1)
    wait(get["up"])
    r.result[...] = dot_nt(r.inner[...], r.up[...])
    wait(get["middle"])

    def rows_step(image, total_gain):
        at = rows_of(cfg, image)
        unit, scale = norm(r.middle[at, :], cfg.true)
        r.normed[at, :] = (unit * r.gain_mlp[...]).astype(HALF)
        here = r.result[at, :]
        full = r.grad[at, :] + norm_back(here * r.gain_mlp[...], unit, scale, cfg.true)
        r.result[at, :] = full
        r.branch[at, :] = full.astype(HALF)
        return total_gain + jnp.sum(here * unit, axis=0, keepdims=True)

    r.gain_mlp_out[...] = lax.fori_loop(0, cfg.images, rows_step, jnp.zeros((1, width), SINGLE), unroll=True)
    if hasattr(r, RESULT):
        copies.put(r.result, r.result_out)
    r.pieces_mlp[0] = dot_tn(r.normed[...], r.inner[...]).astype(HALF)
    put(0)


def attention_back(cfg, r, image):
    rows, width = cfg.rows, cfg.width
    size = cfg.true // HEADS
    scale = size ** (-0.5)
    base = pl.multiple_of(image * rows, 16)
    at = pl.ds(base, rows)
    window = pl.ds(base, WINDOW)
    work = []
    for block in range(width // LANES):
        low = block * LANES
        value = r.mixed[at, 2 * width + low : 2 * width + low + LANES]
        grad_head = r.grad_heads[window, low : low + LANES]
        for head in heads_of(cfg, block)[1]:
            masked = jnp.where(lane_mask(head, size), value, jnp.zeros_like(value))
            work.append(dot_nt(masked, grad_head))
    order = 0
    for block in range(width // LANES):
        low = block * LANES
        query = r.mixed[window, low : low + LANES]
        key_t = r.mixed[at, width + low : width + low + LANES].T
        grad_head = r.grad_heads[window, low : low + LANES]
        here = heads_of(cfg, block)[1]
        grad_key = jnp.zeros((rows, LANES), SINGLE)
        grad_value = jnp.zeros((rows, LANES), SINGLE)
        parts = []
        for head in here:
            mask = lane_mask(head, size)
            grad_prob = work[order]
            order += 1
            prob = r.probs[image * HEADS + head]
            wide = prob.astype(SINGLE)
            along = jnp.sum(wide * grad_prob, axis=0, keepdims=True)
            grad_score = (wide * (grad_prob - along)).astype(HALF)
            grad_value = jnp.where(mask, dot(prob, grad_head), grad_value)
            grad_key = jnp.where(mask, dot(grad_score, query), grad_key)
            first = head * size % LANES
            parts.append(dot(key_t[first : first + size], grad_score))
        if len(here) * size < LANES:
            parts.append(jnp.zeros((LANES - len(here) * size, WINDOW), SINGLE))
        grad_query = jnp.concatenate(parts, axis=0).T[:rows]
        r.grad_mixed[at, low : low + LANES] = (grad_query * scale).astype(HALF)
        r.grad_mixed[at, width + low : width + low + LANES] = (grad_key * scale).astype(HALF)
        r.grad_mixed[at, 2 * width + low : 2 * width + low + LANES] = grad_value.astype(HALF)


def backward_attn(cfg, r, copies, get, last):
    rows, width = cfg.rows, cfg.width
    total = cfg.images * rows
    first_row = r.first_row
    if get["result"]:
        wait(get["result"])
        r.branch[...] = r.result[...].astype(HALF)
    wait(get["out"])
    r.grad_heads[0:total, :] = dot_nt(r.branch[...], r.out[...]).astype(HALF)
    r.grad_heads[total:, :] = jnp.zeros((r.grad_heads.shape[0] - total, width), HALF)

    def fill(index, value):
        value = value.astype(HALF)
        if cfg.true == width:
            r.pieces_attn[index * width : (index + 1) * width, :] = value
        else:
            pack_square(cfg, index, value, r.pieces_attn, 0)

    wait(get[HEADS_AXIS])
    fill(3, dot_tn(r.heads[...], r.branch[...]))
    wait(get["mixed"] + get["probs"])

    @pl.loop(0, cfg.images // BACKWARD_UNROLL)
    def _(step):
        for part in range(BACKWARD_UNROLL):
            attention_back(cfg, r, step * BACKWARD_UNROLL + part)

    wait(get["qkv"])
    r.grad_x[...] = dot_nt(r.grad_mixed[...], r.qkv[...])
    wait(get["x"])

    def rows_step(image, total_gain):
        at = rows_of(cfg, image)
        unit, scale = norm(r.x[at, :], cfg.true)
        r.normed[at, :] = (unit * r.gain_attn[...]).astype(HALF)
        here = r.grad_x[at, :]
        r.grad_x[at, :] = r.result[at, :] + norm_back(here * r.gain_attn[...], unit, scale, cfg.true)
        return total_gain + jnp.sum(here * unit, axis=0, keepdims=True)

    r.gain_attn_out[...] = lax.fori_loop(0, cfg.images, rows_step, jnp.zeros((1, width), SINGLE), unroll=True)
    if last:
        for image in range(cfg.images):
            first = image * rows
            put_tokens(cfg, r.grad_x_out, image, r.grad_x[first : first + rows, :])
    else:
        copies.put(r.grad_x, r.grad_x_out)
    for part in range(3):
        cols = slice(part * width, (part + 1) * width)
        fill(part, dot_tn(r.normed[...], r.grad_mixed[:, cols]))
    put_rows(r.place, r.pieces_attn, 0, r.keep_out, r.send_out, first_row, copies, first_row == 0)
    if hasattr(r, "lines"):
        put_lines(r, copies, first_row + r.pieces_attn.shape[0] // 8)


def backward_body(cfg, layer, attn, mlp, last, first_row, r):
    pick_layer(layer, r)
    copies = Copies(r.semaphores)
    r.first_row = first_row
    get = {"result": []}

    def begin(name):
        get[name] = [copies.begin(getattr(r, name + "_in"), getattr(r, name))]

    if mlp:
        shards = (r.own, r.core, r.far, r.both)
        begin("grad")
        get["down"] = shard_copies(cfg, copies, shards, r.down, 1)
        begin("slope")
        begin("active")
        get["up"] = shard_copies(cfg, copies, shards, r.up, 0)
        begin("middle")
    else:
        begin("result")
    if attn:
        for name in ("out", HEADS_AXIS, "mixed", "probs", "qkv", "x"):
            begin(name)
    if mlp:
        backward_mlp(cfg, r, copies, get)
    if attn:
        backward_attn(cfg, r, copies, get, last)
    copies.finish()


def put_rows(place, source, begin, keep, send, first, copies, side_first=False):
    size = (source.shape[0] - begin) // 8
    outer, inner = (1, 2) if side_first else (2, 1)
    for index in range(8):
        rows = source.at[begin + index * size : begin + (index + 1) * size]
        chunk = 2 * lax.rem(place[outer] + index // 2 % 2, 2) + lax.rem(place[inner] + index % 2, 2)
        semaphore = copies.semaphores.at[copies.block(1)]
        kept = pltpu.make_async_copy(rows, keep.at[chunk, first : first + size], semaphore)
        sent = pltpu.make_async_copy(rows, send.at[chunk, first : first + size], semaphore)
        pl.when(place[3] == index // 4)(kept.start)
        pl.when(place[3] != index // 4)(sent.start)
        copies.puts.append(kept)


def put_lines(r, copies, first):
    r.ready[...] = jnp.zeros(r.ready.shape, SINGLE)
    count = r.lines.shape[0] // 8
    own = r.gain_attn_out[...]
    for index in range(8):
        here = r.lines[index * count : (index + 1) * count, :]
        if index == 0:
            here = here + jnp.where(iota((count, 1), 0) == 0, own, 0.0)
        chunk = 2 * lax.rem(r.place[1] + index // 2 % 2, 2) + lax.rem(r.place[2] + index % 2, 2)
        other = lax.rem(r.place[3] + index // 4, 2)
        r.ready[other, chunk, 0:count, :] = here
    r.lines_half[...] = r.ready[...].astype(HALF)
    for index, target in enumerate((r.keep_out, r.send_out)):
        for chunk in range(4):
            copies.put(r.lines_half.at[index, chunk], target.at[chunk, first : first + LINE_ROWS])


def pack_square(cfg, index, piece, target, first):
    true = cfg.true
    row = first + index // 2 * true
    col = index % 2 * true
    target[row : row + true, col : col + true] = piece[0:true, 0:true]


ANY = pl.BlockSpec(memory_space=pl.ANY)
NEAR = pl.BlockSpec(memory_space=pltpu.VMEM)
SCALAR = pl.BlockSpec(memory_space=pltpu.SMEM)


def shape(dims, dtype):
    return jax.ShapeDtypeStruct(dims, dtype)


def call(name, kernel, in_specs, outs, out_specs, scratch, flops, moved):
    return pl.pallas_call(
        kernel,
        name=name,
        out_shape=outs,
        in_specs=in_specs,
        out_specs=out_specs,
        scratch_shapes=scratch,
        compiler_params=pltpu.CompilerParams(vmem_limit_bytes=VMEM_BYTES),
        cost_estimate=pl.CostEstimate(flops=flops, bytes_accessed=moved, transcendentals=0),
    )


def named_call(name, body, ins, outs, scratch, flops, aliases=()):
    names = [entry[0] for entry in ins + outs + scratch]
    positions = {entry[0]: index for index, entry in enumerate(ins)}
    places = {entry[0]: index for index, entry in enumerate(outs)}

    def kernel(*refs):
        body(types.SimpleNamespace(**dict(zip(names, refs))))

    results = pl.pallas_call(
        kernel,
        name=name,
        out_shape=[entry[1] for entry in outs],
        in_specs=[entry[2] for entry in ins],
        out_specs=[entry[2] for entry in outs],
        scratch_shapes=[entry[1] for entry in scratch],
        input_output_aliases={positions[source]: places[target] for source, target in aliases},
        compiler_params=pltpu.CompilerParams(vmem_limit_bytes=VMEM_BYTES),
        cost_estimate=pl.CostEstimate(flops=flops, bytes_accessed=10**7, transcendentals=0),
    )(*[entry[1] for entry in ins])
    return {entry[0]: result for entry, result in zip(outs, results)}


def sizes(cfg):
    total = cfg.images * cfg.rows
    return total, total + WINDOW - cfg.rows, cfg.width


def semaphores(count):
    return pltpu.SemaphoreType.DMA((count,))


def block_shapes(cfg):
    total, longer, width = sizes(cfg)
    wide = shape((total, width), SINGLE)
    narrow = shape((total, width), HALF)
    inner = shape((total, cfg.hidden), HALF)
    return {
        "x": wide,
        "middle": wide,
        "y": wide,
        "grad": wide,
        "result": wide,
        "grad_x": wide,
        "mixed": shape((longer, 3 * width), HALF),
        "probs": shape((cfg.images * HEADS, cfg.rows, WINDOW), HALF),
        HEADS_AXIS: narrow,
        "normed": narrow,
        "branch": narrow,
        "active": inner,
        "slope": inner,
        "inner": inner,
        "grad_heads": shape((longer, width), HALF),
        "grad_mixed": shape((total, 3 * width), HALF),
        "qkv": shape((width, 3 * width), HALF),
        "out": shape((width, width), HALF),
        "up": shape((width, cfg.hidden), HALF),
        "down": shape((cfg.hidden, width), HALF),
        "pieces_mlp": shape((2, width, cfg.hidden), HALF),
        "pieces_attn": shape((4 * width, width) if cfg.true == width else (2 * cfg.true, 2 * cfg.true), HALF),
        "packed": shape((4, cfg.true, 2 * cfg.true), HALF),
        "ready": shape((2, 4, LINE_ROWS, width), SINGLE),
        "lines_half": shape((2, 4, LINE_ROWS, width), HALF),
        "landing": shape(tokens_shape(cfg), HALF),
    }


def block_call(name, cfg, body, ins, outs, scratch, aliases=()):
    shapes = block_shapes(cfg)
    names = list(dict.fromkeys(scratch))
    scratch = [(entry, pltpu.VMEM(shapes[entry].shape, shapes[entry].dtype)) for entry in names]
    scratch.append(("semaphores", semaphores(56)))
    outs = [entry if len(entry) == 3 else (entry[0], shapes[entry[0][:-4]], ANY) for entry in outs]
    flops = (20 if name == "forward" else 40) * cfg.images * cfg.rows * cfg.width**2
    return named_call(name, body, ins, outs, scratch, flops, aliases)


def shard_ins(shards):
    return [(name, shard, ANY) for name, shard in zip(("own", "core", "far", "both"), shards)]


def block_forward(cfg, x, params, shards=None, place=None, middle=None):
    layer, gain_attn, qkv, out, gain_mlp = params
    attn, mlp = middle is None, shards is not None
    ins, outs, scratch = [], [], []
    if attn:
        ins += [("gain_attn", gain_attn, NEAR), ("qkv_in", qkv, ANY), ("out_in", out, ANY)]
        if place is None:
            ins.append(("x_in", x, ANY))
        else:
            ins += [("tokens", x, ANY), ("place", place, SCALAR)]
            outs.append(("x_out",))
            scratch.append("landing")
        outs += [(MIDDLE,), ("mixed_out",), ("probs_out",), ("heads_out",)]
        scratch += ["x", "qkv", "out", "mixed", "probs", HEADS_AXIS, "normed"]
    else:
        ins.append(("middle_in", middle, ANY))
    if mlp:
        ins += [("gain_mlp", gain_mlp, NEAR)] + shard_ins(shards)
        outs += [(Y_OUT,), ("active_out",), ("slope_out",)]
        scratch += ["up", "down", "active", "slope", "y"]
    scratch.append("middle")
    kept = block_call("forward", cfg, functools.partial(forward_body, cfg, layer, attn, mlp), ins, outs, scratch)
    if attn and place is None:
        kept["x_out"] = x
    if not attn:
        kept[MIDDLE] = middle
    return kept


def block_backward(cfg, place, grad, kept, params, shards, attn=True, mlp=True, last=False, lines=None):
    layer, gain_attn, qkv, out, gain_mlp = params
    packed = cfg.true != cfg.width
    ins, outs, scratch = [("place", place, SCALAR)], [], ["result", "branch", "normed"]
    rows = 0
    if mlp:
        ins += [("grad_in", grad, ANY), ("gain_mlp", gain_mlp, NEAR)] + shard_ins(shards)
        ins += [(name + "_in", kept[name + "_out"], ANY) for name in ("middle", "active", "slope")]
        outs.append((GAIN_MLP, shape((1, cfg.width), SINGLE), NEAR))
        scratch += ["grad", "middle", "active", "slope", "up", "down", "inner", "pieces_mlp"]
        scratch += ["packed"] if packed else []
        rows += cfg.true // 2 if packed else cfg.width
        if not attn:
            outs.append((RESULT,))
    first_row = rows
    if attn:
        ins += [("gain_attn", gain_attn, NEAR), ("qkv_in", qkv, ANY), ("out_in", out, ANY)]
        ins += [(name + "_in", kept[name + "_out"], ANY) for name in ("x", "mixed", "probs", HEADS_AXIS)]
        if not mlp:
            ins.append(("result_in", grad, ANY))
        outs.append((GAIN_ATTN, shape((1, cfg.width), SINGLE), NEAR))
        if last:
            outs.append((GRAD_X, shape(tokens_shape(cfg), HALF), NEAR))
        else:
            outs.append((GRAD_X,))
        rows += cfg.true // 4 if packed else cfg.width // 2
        scratch += ["x", "mixed", "probs", HEADS_AXIS, "qkv", "out", "grad_heads", "grad_mixed", "grad_x", "pieces_attn"]
        if lines is not None:
            ins.append(("lines", lines, NEAR))
            scratch += ["ready", "lines_half"]
            rows += LINE_ROWS
    chunk = shape((4, rows, 2 * cfg.true if packed else cfg.width), HALF)
    outs += [(KEEP, chunk, ANY), (SEND, chunk, ANY)]
    body = functools.partial(backward_body, cfg, layer, attn, mlp, last, first_row)
    return block_call("backward", cfg, body, ins, outs, scratch)


def class_rows(ref, cfg):
    rows = [ref[image * cfg.rows : image * cfg.rows + 1, :] for image in range(cfg.images)]
    rows.append(jnp.zeros((CLS_ROWS - cfg.images, ref.shape[1]), ref.dtype))
    return jnp.concatenate(rows, axis=0)


def pack_rows(rows, images):
    rows.append(jnp.zeros((CLS_ROWS - images, rows[0].shape[1]), rows[0].dtype))
    return jnp.concatenate(rows, axis=0)


def unite_part(
    own, other, own_ref, other_ref, own_cot, weights, grads, unit, normed, keyval, grad_keyval, grad_patch
):
    gain_in, lift, gain_attn, qkv, out, gain_back, revert = weights
    g_in, g_attn, g_back, pack = grads
    images, rows, width = other.images, other.rows, other.width
    own_small = own.true < other.true
    total = images * rows
    size = other.true // HEADS
    scale = size ** (-0.5)
    lane = iota((CLS_ROWS, width), 1)
    head_low = iota((CLS_ROWS, width), 0) * size
    head_mask = ((lane >= head_low) & (lane < head_low + size) & (lane < other.true)).astype(SINGLE)
    key_ok = iota((CLS_ROWS, WINDOW), 1) < other.length

    unit_in, scale_in = norm(class_rows(own_ref, own), own.true)
    lifted_in, slope_in = gelu_both(unit_in * gain_in[...])
    lifted_in = lifted_in.astype(HALF)
    lifted = dot(lifted_in, lift[...])
    unit_cls, scale_cls = norm(lifted, other.true)
    normed_cls = (unit_cls * gain_attn[...]).astype(HALF)

    for image in range(images):
        at = slice(image * rows, (image + 1) * rows)
        here = jnp.where(
            iota((rows, 1), 0) == 0, lifted[image : image + 1], other_ref[at, :]
        )
        unit_here, scale_here = norm(here, other.true)
        unit[at, :] = unit_here
        grad_patch[at, :] = jnp.broadcast_to(scale_here, (rows, width))
        normed[at, :] = (unit_here * gain_attn[...]).astype(HALF)

    for part in range(2):
        cols = slice(part * width, (part + 1) * width)
        keyval[0:total, cols] = dot(
            normed[...], qkv[:, (part + 1) * width : (part + 2) * width]
        ).astype(HALF)
    keyval[total:, :] = jnp.zeros((keyval.shape[0] - total, 2 * width), HALF)
    query = dot(normed_cls, qkv[:, 0:width]).astype(HALF).astype(SINGLE)
    queries, probs_all, probs_half, merged = [], [], [], []
    for image in range(images):
        window = slice(image * rows, image * rows + WINDOW)
        spread = (head_mask * query[image : image + 1]).astype(HALF)
        scores = dot_nt(spread, keyval[window, 0:width]) * scale
        scores = jnp.where(key_ok, scores, NEG)
        raised = jnp.exp(scores - jnp.max(scores, axis=1, keepdims=True))
        prob = raised / jnp.sum(raised, axis=1, keepdims=True)
        half = prob.astype(HALF)
        mixed = dot(half, keyval[window, width : 2 * width])
        merged.append(jnp.sum(mixed * head_mask, axis=0, keepdims=True))
        queries.append(spread)
        probs_all.append(prob)
        probs_half.append(half)
    merged = pack_rows(merged, images).astype(HALF)
    calibrated = lifted + dot(merged, out[...])
    unit_back, scale_back = norm(calibrated, other.true)
    back_in, slope_back = gelu_both(unit_back * gain_back[...])
    back_in = back_in.astype(HALF)
    result = dot(back_in, revert[...])

    grad_final = class_rows(own_cot, own).astype(HALF)
    g_revert = dot_tn(grad_final, back_in) if own_small else dot_tn(back_in, grad_final)
    grad_back = dot_nt(grad_final, revert[...]) * slope_back
    g_back[...] = jnp.sum(grad_back * unit_back, axis=0, keepdims=True)
    grad_cal = norm_back(grad_back * gain_back[...], unit_back, scale_back, other.true)
    grad_cross = grad_cal.astype(HALF)
    g_out = dot_tn(merged, grad_cross).astype(HALF)
    grad_merged = dot_nt(grad_cross, out[...]).astype(HALF).astype(SINGLE)
    grad_query = []
    for image in range(images):
        window = slice(image * rows, image * rows + WINDOW)
        at = slice(image * rows, (image + 1) * rows)
        spread = (head_mask * grad_merged[image : image + 1]).astype(HALF)
        grad_prob = dot_nt(spread, keyval[window, width : 2 * width])
        prob = probs_all[image]
        along = jnp.sum(prob * grad_prob, axis=1, keepdims=True)
        grad_score = (prob * (grad_prob - along)).astype(HALF)
        back = dot(grad_score, keyval[window, 0:width]) * head_mask
        grad_query.append(jnp.sum(back, axis=0, keepdims=True) * scale)
        grad_key = dot_tn(grad_score, queries[image]) * scale
        grad_value = dot_tn(probs_half[image], spread)
        grad_keyval[at, 0:width] = grad_key[:rows].astype(HALF)
        grad_keyval[at, width : 2 * width] = grad_value[:rows].astype(HALF)
    grad_query = pack_rows(grad_query, images).astype(HALF)
    g_qkv = [dot_tn(normed_cls, grad_query).astype(HALF)]
    for part in range(2):
        cols = slice(part * width, (part + 1) * width)
        g_qkv.append(dot_tn(normed[...], grad_keyval[:, cols]).astype(HALF))
    from_query = dot_nt(grad_query, qkv[:, 0:width])
    gain_total = jnp.zeros((1, width), SINGLE)
    grad_lifted = []
    for image in range(images):
        at = slice(image * rows, (image + 1) * rows)
        grad = dot_nt(grad_keyval[at, :], qkv[:, width : 3 * width])
        grad = grad + jnp.where(iota((rows, 1), 0) == 0, from_query[image : image + 1], 0.0)
        unit_here = unit[at, :]
        gain_total = gain_total + jnp.sum(grad * unit_here, axis=0, keepdims=True)
        scale_here = grad_patch[at, :]
        back = norm_back(grad * gain_attn[...], unit_here, scale_here, other.true)
        grad_patch[at, :] = back
        grad_lifted.append(back[0:1])
    g_attn[...] = gain_total
    grad_lifted = (grad_cal + pack_rows(grad_lifted, images)).astype(HALF)
    g_lift = dot_tn(lifted_in, grad_lifted) if own_small else dot_tn(grad_lifted, lifted_in)
    grad_in = dot_nt(grad_lifted, lift[...]) * slope_in
    g_in[...] = jnp.sum(grad_in * unit_in, axis=0, keepdims=True)
    grad_cls = norm_back(grad_in * gain_in[...], unit_in, scale_in, own.true)
    narrow = min(own.true, other.true)
    wide = max(own.true, other.true)
    target, row = pack
    for piece in (g_lift, g_revert):
        target[row : row + narrow, :] = piece[0:narrow, :].astype(HALF)
        row += narrow
    if own_small:
        for piece in g_qkv + [g_out]:
            target[row : row + wide, :] = piece
            row += wide
    else:
        for index, piece in enumerate(g_qkv + [g_out]):
            pack_square(other, index, piece, target, row)
    return result, grad_cls


def finish_rows(cfg, mid_ref, cot_ref, result, grad_cls, result_ref, grad_ref):
    for image in range(cfg.images):
        at = slice(image * cfg.rows, (image + 1) * cfg.rows)
        first = iota((cfg.rows, 1), 0) == 0
        rows = jnp.where(first, result[image : image + 1], mid_ref[at, :])
        put_tokens(cfg, result_ref, image, rows)
        grad_ref[at, :] = jnp.where(
            first, grad_cls[image : image + 1], grad_ref[at, :] + cot_ref[at, :]
        )


def unite_rows(small, large):
    first = 2 * small.true + 4 * large.true
    used = first + 4 * small.true
    return first, used, round_up(used, 512)


def unite_kernel(small, large, *refs):
    place, small_tokens, large_tokens, small_mid, large_mid = refs[0:5]
    first, second = refs[5:12], refs[12:19]
    small_res, large_res, grad_small, grad_large, keep, send = refs[19:25]
    first_gains, second_gains = refs[25:28], refs[28:31]
    first_work, second_work = refs[31:35], refs[35:39]
    small_land, large_land, small_cot, large_cot, packed, sems = refs[39:]
    begin, used, rows = unite_rows(small, large)
    copies = Copies(sems)
    load_tokens(small, place, small_tokens, small_land, small_cot, copies)
    load_tokens(large, place, large_tokens, large_land, large_cot, copies)
    packed[used:rows, :] = jnp.zeros((rows - used, packed.shape[1]), HALF)
    small_head, grad_small_cls = unite_part(
        small, large, small_mid, large_mid, small_cot, first, (*first_gains, (packed, 0)), *first_work, grad_large
    )
    large_head, grad_large_cls = unite_part(
        large, small, large_mid, small_mid, large_cot, second, (*second_gains, (packed, begin)), *second_work,
        grad_small,
    )
    put_rows(place, packed, 0, keep, send, 0, copies)
    finish_rows(small, small_mid, small_cot, small_head, grad_small_cls, small_res, grad_small)
    finish_rows(large, large_mid, large_cot, large_head, grad_large_cls, large_res, grad_large)
    copies.finish()


def unite_both(small, large, place, small_cot, large_cot, small_mid, large_mid, first, second):
    def gains(own, other):
        return [shape((1, own.width), SINGLE), shape((1, other.width), SINGLE), shape((1, other.width), SINGLE)]

    def work(other):
        total, longer, width = sizes(other)
        return [
            pltpu.VMEM((total, width), SINGLE),
            pltpu.VMEM((total, width), HALF),
            pltpu.VMEM((longer, 2 * width), HALF),
            pltpu.VMEM((total, 2 * width), HALF),
        ]

    def rows(cfg):
        return shape((cfg.images * cfg.rows, cfg.width), SINGLE)

    def tokens(cfg):
        return shape(tokens_shape(cfg), HALF)

    outs = [tokens(small), tokens(large), rows(small), rows(large)]
    packed = unite_rows(small, large)[2]
    outs += [shape((4, packed // 8, large.width), HALF)] * 2
    outs += gains(small, large) + gains(large, small)
    scratch = work(large) + work(small)
    for cfg in (small, large):
        scratch.append(pltpu.VMEM(tokens_shape(cfg), HALF))
    for cfg in (small, large):
        scratch.append(pltpu.VMEM((cfg.images * cfg.rows, cfg.width), SINGLE))
    scratch += [pltpu.VMEM((packed, large.width), HALF), semaphores(10)]
    return call(
        "unite", functools.partial(unite_kernel, small, large), [SCALAR, ANY, ANY] + [NEAR] * 16, outs,
        [NEAR] * 4 + [ANY] * 2 + [NEAR] * 6, scratch, 30 * large.images * large.rows * large.width**2, 10**7,
    )(place, small_cot, large_cot, small_mid, large_mid, *first, *second)


def pad_dims(array, dims):
    return jnp.pad(array, [(0, dim - old) for old, dim in zip(array.shape, dims)])


def prepare_kernel(small, large, *refs):
    ins, outs, up, down, sems = refs[0:20], refs[20:-3], refs[-3], refs[-2], refs[-1]
    stacked = outs[17:]
    copies = Copies(sems)
    gets = []
    for layer in range(len(stacked)):
        gets.append(copies.begin(ins[18].at[layer], up.at[layer]))
        gets.append(copies.begin(ins[19].at[layer], down.at[layer]))
    for layer, target in enumerate(stacked):
        gets[2 * layer].wait()
        copies.put(up.at[layer], target.at[0])
        gets[2 * layer + 1].wait()
        copies.put(down.at[layer], target.at[1])
    shard = outs[16]
    shard[...] = jnp.zeros(shard.shape, HALF)
    for index in range(2):
        matrix = ins[16 + index]
        shard[index, 0 : matrix.shape[0], 0 : matrix.shape[1]] = matrix[...]
    for source, target in zip(ins[0:16], outs[0:16]):
        tall, wide = source.shape
        target[...] = jnp.zeros(target.shape, target.dtype)
        if wide == 3 * small.true and tall == small.true:
            for part in range(3):
                cols = slice(part * small.width, part * small.width + tall)
                target[0:tall, cols] = source[:, part * tall : (part + 1) * tall]
        elif tall == small.true and target.shape[0] == large.width:
            target[0:wide, 0:tall] = source[...].astype(SINGLE).T.astype(target.dtype)
        else:
            target[0:tall, 0:wide] = source[...]
    copies.finish()


def prepare(small, large, small_params, first, second, large_up, large_down):
    gain_attn, qkv, out, gain_mlp, up, down = small_params
    depth = large_up.shape[0]
    ns, nl = small.width, large.width
    squares = [gain_attn[None], qkv, out, gain_mlp[None]]
    sizes_out = [(1, ns), (ns, 3 * ns), (ns, ns), (1, ns)]

    def unite_pads(weights, own, other):
        gain_in, lift, gain, qkv, out, gain_back, revert = weights
        lift, revert = [matrix.T if matrix.shape[0] > matrix.shape[1] else matrix for matrix in (lift, revert)]
        arrays = [gain_in[None], lift, gain[None], out, gain_back[None], revert]
        shapes = [(1, own), (own, other), (1, other), (other, other), (1, other), (other, own)]
        return arrays, shapes, qkv, (other, 3 * other)

    first_arrays, first_shapes, first_qkv, _ = unite_pads(first, ns, nl)
    second_arrays, second_shapes, second_qkv, second_dims = unite_pads(second, nl, ns)
    need = [0, 1, 5]
    arrays = squares + [first_arrays[index] for index in need] + second_arrays + [second_qkv]
    dims = sizes_out + [first_shapes[index] for index in need] + second_shapes + [second_dims]
    extra = 16 - len(arrays)
    arrays += [gain_attn[None]] * extra
    dims += [(1, ns)] * extra
    outs = [shape(size, array.dtype) for size, array in zip(dims, arrays)]
    outs += [shape((2, ns, small.hidden // 4), HALF)]
    outs += [shape((2, nl, nl), HALF)] * depth
    results = call(
        "prepare", functools.partial(prepare_kernel, small, large), [NEAR] * 18 + [ANY] * 2, outs,
        [NEAR] * 17 + [ANY] * depth,
        [pltpu.VMEM(large_up.shape, HALF), pltpu.VMEM(large_down.shape, HALF), semaphores(4 * depth)], 10**6, 10**7,
    )(*arrays, up, down, large_up, large_down)
    small_ready = results[0:4]
    f_in, f_lift, f_revert = results[4:7]
    s_in, s_lift, s_attn, s_out, s_back, s_revert, s_qkv = results[7:14]
    first_ready = (f_in, f_lift, first_arrays[2], first_qkv, first_arrays[3], first_arrays[4], f_revert)
    second_ready = (s_in, s_lift, s_attn, s_qkv, s_out, s_back, s_revert)
    return small_ready, first_ready, second_ready, results[16], results[17:]


def plus(*terms):
    total = terms[0].astype(SINGLE)
    for term in terms[1:]:
        total = total + term.astype(SINGLE)
    return total.astype(HALF)


class Links:
    def __init__(self):
        heads, dp = lax.axis_size(HEADS_AXIS), lax.axis_size(ROW_AXIS)
        place, row = lax.axis_index(HEADS_AXIS), lax.axis_index(ROW_AXIS)
        self.heads, self.dp = heads, dp
        self.core, self.far, self.side = place % 2, place // 2, row % 2

    def scalars(self):
        place = lax.axis_index(HEADS_AXIS)
        return jnp.stack([place, self.side, self.far, self.core]).astype(jnp.int32)

    def swap(self, array, axis, bit):
        size = self.heads if axis == HEADS_AXIS else self.dp
        return lax.ppermute(array, axis, [(index, index ^ bit) for index in range(size)])

    def by_core(self, array):
        return self.swap(array, HEADS_AXIS, 1)

    def by_far(self, array):
        return self.swap(array, HEADS_AXIS, 2)

    def by_side(self, array):
        return self.swap(array, ROW_AXIS, 1)

    def long_steps(self):
        bits = [2 << step for step in range((self.dp // 2).bit_length() - 1)]
        if len(bits) == 2:
            bits = [2, 6]
        return [functools.partial(self.swap, axis=ROW_AXIS, bit=bit) for bit in bits]


def whole(mine, other, index):
    return jnp.where(index == 0, jnp.stack([mine, other]), jnp.stack([other, mine]))


def reduce_steps(links, keep, send, shared, side_first=False):
    owned = keep.shape[1] - shared
    lanes = keep.shape[2]
    outer, inner = (links.by_far, links.far), (links.by_side, links.side)
    if side_first:
        outer, inner = inner, outer
    (send,) = yield [send]
    got = links.by_core(send)
    away, own = yield [plus(keep[2:4], got[2:4]), plus(keep[0:2], got[0:2])]
    got = outer[0](away)
    away, own = yield [plus(own[1], got[1]), plus(own[0], got[0])]
    (own,) = yield [plus(own, inner[0](away))]
    for step in links.long_steps():
        (own,) = yield [plus(own, step(own))]
    got = inner[0](own)
    hidden = whole(own[:owned], got[:owned], inner[1]) if owned else None
    if not shared:
        return hidden, None
    (mine,) = yield [whole(own[owned:], got[owned:], inner[1]).reshape(-1, lanes)]
    (mine,) = yield [whole(mine, outer[0](mine), outer[1]).reshape(-1, lanes)]
    return hidden, whole(mine, links.by_core(mine), links.core).reshape(-1, lanes)


class Rounds:
    def __init__(self):
        self.active = {}
        self.waiting = {}
        self.done = {}

    def add(self, name, steps):
        self.active[name] = steps
        self.waiting[name] = next(steps)

    def tie(self, names, *arrays):
        names = [name for name in (self.active if names is None else names) if name in self.active]
        held = {name: self.waiting[name] for name in names}
        if held:
            arrays, held = lax.optimization_barrier((arrays, held))
        for name in names:
            try:
                self.waiting[name] = self.active[name].send(held[name])
            except StopIteration as stop:
                self.done[name] = stop.value
                del self.active[name], self.waiting[name]
        return arrays if len(arrays) != 1 else arrays[0]


def per_device(
    small_tokens,
    large_tokens,
    small_cotangent,
    large_cotangent,
    small_gain_attn,
    small_qkv,
    small_out,
    small_gain_mlp,
    small_up,
    small_down,
    large_gain_attn,
    large_qkv,
    large_out,
    large_gain_mlp,
    large_up,
    large_down,
    *unite_weights,
):
    devices = lax.axis_size(HEADS_AXIS)
    depth = large_qkv.shape[0]
    images = small_tokens.shape[0] // devices
    links = Links()
    place = links.scalars()

    def branch(tokens, hidden):
        _, length, true = tokens.shape
        return Branch(images, round_up(length, 16), length, round_up(true, LANES), true, hidden * devices)

    small = branch(small_tokens, round_up(small_up.shape[1], LANES))
    large = branch(large_tokens, large_up.shape[2])
    small_ready, first, second, small_shard, large_shards = prepare(
        small,
        large,
        (small_gain_attn, small_qkv, small_out, small_gain_mlp, small_up, small_down),
        unite_weights[0:7],
        unite_weights[7:14],
        large_up,
        large_down,
    )

    def after(value, *others):
        return lax.optimization_barrier((value, *others))[0]

    def spread(shard, far):
        return (shard, links.by_core(shard), far, links.by_core(far))

    far_small = links.by_far(small_shard)
    far = [links.by_far(large_shards[0])]
    large_gains = [(large_gain_attn[layer][None], large_gain_mlp[layer][None]) for layer in range(depth)]

    small_block = (None, *small_ready[0:4])
    large_blocks = [
        (layer, large_gains[layer][0], large_qkv, large_out, large_gains[layer][1]) for layer in range(depth)
    ]
    small_tokens, small_cotangent = small_tokens.swapaxes(1, 2), small_cotangent.swapaxes(1, 2)
    small_kept = block_forward(small, small_tokens, small_block, None, place)
    tokens, small_kept[MIDDLE] = lax.optimization_barrier((large_tokens, small_kept[MIDDLE]))
    large_kept, large_weights = [], []
    kept = block_forward(large, tokens, large_blocks[0], None, place)
    small_middle, middle, far[0], far_small = lax.optimization_barrier(
        (small_kept[MIDDLE], kept[MIDDLE], far[0], far_small)
    )
    small_weights = spread(small_shard, far_small)
    large_weights.append(spread(large_shards[0], far[0]))
    far.append(links.by_far(after(large_shards[1], far[0])))
    small_kept |= block_forward(small, None, small_block, small_weights, None, small_middle)
    middle = after(middle, small_kept[Y_OUT])
    kept |= block_forward(large, None, large_blocks[0], large_weights[0], None, middle)
    large_kept.append(kept)
    state = kept[Y_OUT]
    for layer in range(1, depth):
        state, far[layer] = lax.optimization_barrier((state, far[layer]))
        large_weights.append(spread(large_shards[layer], far[layer]))
        if layer + 1 < depth:
            far.append(links.by_far(after(large_shards[layer + 1], far[layer])))
        large_kept.append(block_forward(large, state, large_blocks[layer], large_weights[layer]))
        state = large_kept[layer][Y_OUT]
    small_mid = small_kept[Y_OUT]

    small_res, large_res, grad_small, grad, keep, send, *unite_gains = unite_both(
        small, large, place, small_cotangent, large_cotangent, small_mid, state, first, second
    )

    def gather(array):
        return lax.all_gather(array, HEADS_AXIS, axis=0, tiled=True)

    small_result, large_result = gather(small_res).swapaxes(1, 2), gather(large_res)
    rounds = Rounds()
    rounds.add("unite", reduce_steps(links, keep, send, keep.shape[1]))
    gains = [None] * depth
    lanes = large.width

    def large_back(layer):
        names = [name for name in rounds.active if layer != 1 or name != "large2"]
        back = block_backward(large, place, rounds.tie(names, grad), large_kept[layer], large_blocks[layer], large_weights[layer])
        gains[layer] = (back[GAIN_ATTN], back[GAIN_MLP])
        rounds.add("large%d" % layer, reduce_steps(links, back[KEEP], back[SEND], lanes // 2))
        return back[GRAD_X]

    for layer in range(depth - 1, 0, -1):
        if layer == 1:
            grad, grad_small = lax.optimization_barrier((grad, grad_small))
            grad_small = rounds.tie(None, grad_small)
            back = block_backward(small, place, grad_small, small_kept, small_block, small_weights, last=True)
            rounds.add("small", reduce_steps(links, back[KEEP], back[SEND], small.true // 4))
            small_grad = gather(back[GRAD_X]).swapaxes(1, 2).astype(SINGLE)
            small_gains = [back[GAIN_ATTN], back[GAIN_MLP]]
            grad, small_gains = lax.optimization_barrier((grad, small_gains))
        grad = large_back(layer)
    grad = rounds.tie(None, grad)
    back = block_backward(large, place, grad, large_kept[0], large_blocks[0], large_weights[0], attn=False)
    rounds.add("hidden0", reduce_steps(links, back[KEEP], back[SEND], 0))
    gains[0] = (jnp.zeros((1, lanes), SINGLE), back[GAIN_MLP])
    lines = [gain for pair in gains for gain in pair] + small_gains + unite_gains
    lines = jnp.concatenate([pad_dims(line, (1, lanes)) for line in lines])
    lines = pad_dims(lines, (round_up(lines.shape[0], 8), lanes))
    grad = rounds.tie(None, back[RESULT])
    back = block_backward(
        large, place, grad, large_kept[0], large_blocks[0], None, mlp=False, last=True, lines=lines
    )
    rounds.add("large0", reduce_steps(links, back[KEEP], back[SEND], lanes // 2 + LINE_ROWS, True))
    large_grad = gather(back[GRAD_X]).astype(SINGLE)
    while rounds.active:
        rounds.tie(None)

    true = small.true

    def square(rows):
        (q, k), (v, o) = [jnp.split(half, 2, axis=1) for half in jnp.split(rows, 2, axis=0)]
        return jnp.concatenate([q, k, v], axis=1), o

    def full(rows):
        q, k, v, o = jnp.split(rows, 4, axis=0)
        return jnp.concatenate([q, k, v], axis=1), o

    s_hidden, s_rest = rounds.done["small"]
    s_hidden = s_hidden.reshape(true, 2 * true).astype(SINGLE)
    s_qkv, s_out = square(s_rest.astype(SINGLE))
    count = lines.shape[0] // 8
    last = rounds.done["large0"][1].reshape(8, -1, lanes)
    line = last[:, lanes // 2 : lanes // 2 + count].reshape(8 * count, lanes).astype(SINGLE)
    first_rest = last[:, : lanes // 2].reshape(4 * lanes, lanes)
    at = 2 * depth
    l_hidden = [rounds.done["large%d" % layer if layer else "hidden0"][0] for layer in range(depth)]
    l_rest = [full(rounds.done["large%d" % layer][1] if layer else first_rest) for layer in range(depth)]
    u_rest = rounds.done["unite"][1].astype(SINGLE)
    begin, used, _ = unite_rows(small, large)
    f_qkv, f_out = full(u_rest[2 * true : begin])
    u_second = u_rest[begin:used]
    e_qkv, e_out = square(u_second[2 * true :])
    return (
        small_result,
        large_result,
        small_grad,
        large_grad,
        line[at, :true],
        s_qkv,
        s_out,
        line[at + 1, :true],
        s_hidden[:, :true],
        s_hidden[:, true:].T,
        line[0:at:2],
        jnp.stack([pair[0] for pair in l_rest]).astype(SINGLE),
        jnp.stack([pair[1] for pair in l_rest]).astype(SINGLE),
        line[1:at:2],
        jnp.stack([pair[0] for pair in l_hidden]).astype(SINGLE),
        jnp.stack([pair[1] for pair in l_hidden]).swapaxes(1, 2).astype(SINGLE),
        line[at + 2, :true],
        u_rest[:true],
        line[at + 3],
        f_qkv,
        f_out,
        line[at + 4],
        u_rest[true : 2 * true].T,
        line[at + 5],
        u_second[:true].T,
        line[at + 6, :true],
        e_qkv,
        e_out,
        line[at + 7, :true],
        u_second[true : 2 * true],
    )


def solution(mesh):
    rows = P(ROW_AXIS, None, None)
    copied = P()
    split = [copied] * 4 + [P(None, HEADS_AXIS), P(HEADS_AXIS, None)]
    stack = [copied] * 4 + [P(None, None, HEADS_AXIS), P(None, HEADS_AXIS, None)]
    specs = tuple([rows] * 4 + split + stack + [copied] * 14)
    return jax.shard_map(per_device, mesh=mesh, in_specs=specs, out_specs=specs, check_vma=False)
```
